256 devices in a mesh: seq: 32 (over z, x_hi, core), dp: 8 (over y, x_lo).
Axes of the slice: x: 4 (x_hi: 2, x_lo: 2; x = x_hi * 2 + x_lo), y: 4, z: 8, core: 2. Of those that a mesh axis runs over, the one named last changes fastest.
Arguments:
- counts: int32 [8, 4096, 64], P('dp', 'seq'), may hold values from 0 to 63
- w_in: bfloat16 [64, 2304], replicated, may hold values from -0.75 to 0.75
- bias_one: float32 [768], replicated, may hold values from -4 to 4
- bias_two: float32 [768], replicated, may hold values from -4 to 4
- filter_one: bfloat16 [768, 4096], P('seq', 'dp'), may hold values from -0.09375 to 0.09375
- filter_two: bfloat16 [768, 4096], P('seq', 'dp'), may hold values from -0.09375 to 0.09375
- cotangent: bfloat16 [8, 768, 4096], P('dp', None, 'seq'), may hold values from -6 to 6
Outputs:
- output: bfloat16 [8, 768, 4096], P('dp', None, 'seq')
- grad_w_in: float32 [64, 2304], replicated
- grad_bias_one: float32 [768], replicated
- grad_bias_two: float32 [768], replicated
- grad_filter_one: bfloat16 [768, 4096], P(('seq', 'dp'))
- grad_filter_two: bfloat16 [768, 4096], P(('seq', 'dp'))
The draws below stay inside these ranges and needn't reach their ends.
All inputs are finite; a program needn't handle non-finite values.
Results may differ from the reference program's by a relative error of at most 0.01.
Values may be sent and summed in bfloat16 or wider, within the bound.
A program may use at most 64 MiB of HBM per device.

```python
import math
import jax
import jax.numpy as jnp
from jax import lax

D = 768
EVENTS = 64
BINS = 4096
STREAMS = 8


def with_ends(result, rng, least, top_value):
    dims = result.shape
    index_at = [jax.random.randint(jax.random.fold_in(rng, axis), (), 0, dims[axis]) for axis in range(len(dims))]
    result = result.at[tuple(index_at)].set(least)
    longest = dims.index(max(dims))
    index_at[longest] = (index_at[longest] + 1) % dims[longest]
    return result.at[tuple(index_at)].set(top_value)


def level_of(key, shape, cuts, smallest, top_value):
    gain = 1.0
    for position, parts in cuts:
        heights = jax.random.uniform(jax.random.fold_in(jax.random.fold_in(key, 6), position), (parts,), jnp.float32, smallest / len(cuts), top_value / len(cuts))
        gain = gain * jnp.repeat(jnp.exp(heights), shape[position] // parts).reshape((-1,) + (1,) * (len(shape) - 1 - position))
    return gain


def bell_draw(stream_key, dims, spread, reach, pieces=(), dtype=jnp.bfloat16):
    level = level_of(stream_key, dims, pieces, -0.22, 0.18) if pieces else 1.0
    result = jax.random.normal(stream_key, dims, jnp.float32) * spread * level
    return jnp.minimum(jnp.maximum(result, -reach), reach).astype(dtype)


def setup_inputs(seed: int = 0) -> dict:
    keys = jax.random.split(jax.random.key(seed), 8)
    return {
        "counts": with_ends(jax.random.randint(keys[0], (STREAMS, BINS, EVENTS), 0, 64), jax.random.fold_in(keys[0], 1), 0, 63).astype(jnp.int32),
        "w_in": bell_draw(keys[1], (EVENTS, 3 * D), EVENTS ** -0.5, 0.75),
        "bias_one": bell_draw(keys[2], (D,), 1.0, 4.0, (), jnp.float32),
        "bias_two": bell_draw(keys[3], (D,), 1.0, 4.0, (), jnp.float32),
        "filter_one": bell_draw(keys[4], (D, BINS), BINS ** -0.5, 0.09375, ((0, 32), (1, 8))),
        "filter_two": bell_draw(keys[5], (D, BINS), BINS ** -0.5, 0.09375, ((0, 32), (1, 8))),
        "cotangent": bell_draw(keys[6], (STREAMS, D, BINS), 1.0, 6.0, ((0, 8), (2, 32))),
    }


count_shift = 3.0

def rounded(values):
    return lax.optimization_barrier(values.astype(jnp.bfloat16)).astype(jnp.float32)

def spectrum(signal):
    return jnp.fft.rfft(signal, n=2 * signal.shape[-1], axis=-1)

def to_signal(spectral, length):
    return jnp.fft.irfft(spectral, n=2 * length, axis=-1)[..., :length]

def reference(counts, w_in, bias_one, bias_two, filter_one, filter_two, cotangent):
    kernel_one = spectrum(filter_one.astype(jnp.float32))
    kernel_two = spectrum(filter_two.astype(jnp.float32))
    skip_one = bias_one[:, None]
    skip_two = bias_two[:, None]
    loss_scale = 1.0 / math.sqrt(STREAMS * BINS)

    def one_stream(carry, inputs):
        stream_counts, stream_cotangent = inputs
        levels = (jnp.log1p(stream_counts.astype(jnp.float32)) - count_shift).astype(jnp.bfloat16)
        projected = lax.dot_general(w_in, levels, (((0,), (1,)), ((), ())), preferred_element_type=jnp.float32)
        value_part = rounded(projected[:D])
        gate_one = rounded(projected[D:2 * D])
        gate_two = rounded(projected[2 * D:])
        value_hat = spectrum(value_part)
        conv_one = rounded(to_signal(kernel_one * value_hat, BINS))
        mixed_one = conv_one + skip_one * value_part
        hidden = rounded(gate_one * mixed_one)
        hidden_hat = spectrum(hidden)
        conv_two = rounded(to_signal(kernel_two * hidden_hat, BINS))
        mixed_two = conv_two + skip_two * hidden
        output = (gate_two * mixed_two).astype(jnp.bfloat16)
        upstream = stream_cotangent.astype(jnp.float32) * loss_scale
        grad_mixed_two = rounded(upstream * gate_two)
        grad_two_hat = spectrum(grad_mixed_two)
        carried_two = rounded(to_signal(jnp.conj(kernel_two) * grad_two_hat, BINS))
        grad_hidden = skip_two * grad_mixed_two + carried_two
        grad_mixed_one = rounded(grad_hidden * gate_one)
        grad_one_hat = spectrum(grad_mixed_one)
        carried_one = rounded(to_signal(jnp.conj(kernel_one) * grad_one_hat, BINS))
        grad_value = skip_one * grad_mixed_one + carried_one
        grad_projected = jnp.concatenate([grad_value, grad_hidden * mixed_one, upstream * mixed_two], axis=0)
        grad_projected = grad_projected.astype(jnp.bfloat16)
        weight_sum, bias_one_sum, bias_two_sum, real_one, imag_one, real_two, imag_two = carry
        weight_sum = weight_sum + lax.dot_general(levels, grad_projected, (((0,), (1,)), ((), ())), preferred_element_type=jnp.float32)
        bias_one_sum = bias_one_sum + lax.optimization_barrier(jnp.sum(grad_mixed_one * value_part, axis=1))
        bias_two_sum = bias_two_sum + lax.optimization_barrier(jnp.sum(grad_mixed_two * hidden, axis=1))
        term_one = jnp.conj(value_hat) * grad_one_hat
        term_two = jnp.conj(hidden_hat) * grad_two_hat
        real_one = real_one + jnp.real(term_one)
        imag_one = imag_one + jnp.imag(term_one)
        real_two = real_two + jnp.real(term_two)
        imag_two = imag_two + jnp.imag(term_two)
        return ((weight_sum, bias_one_sum, bias_two_sum, real_one, imag_one, real_two, imag_two), output)
    start = (jnp.zeros((EVENTS, 3 * D), jnp.float32), jnp.zeros((D,), jnp.float32), jnp.zeros((D,), jnp.float32), jnp.zeros((D, BINS + 1), jnp.float32), jnp.zeros((D, BINS + 1), jnp.float32), jnp.zeros((D, BINS + 1), jnp.float32), jnp.zeros((D, BINS + 1), jnp.float32))
    final, outputs = lax.scan(one_stream, start, (counts, cotangent))
    weight_sum, bias_one_sum, bias_two_sum, real_one, imag_one, real_two, imag_two = final
    grad_filter_one = to_signal(lax.complex(real_one, imag_one), BINS).astype(jnp.bfloat16)
    grad_filter_two = to_signal(lax.complex(real_two, imag_two), BINS).astype(jnp.bfloat16)
    return (outputs, weight_sum, bias_one_sum, bias_two_sum, grad_filter_one, grad_filter_two)
```

```python
import functools
import math

import jax
import jax.numpy as jnp
import numpy as np
from jax import lax
from jax.experimental import pallas as pl
from jax.experimental.pallas import tpu as pltpu
from jax.sharding import PartitionSpec as P

SEQ = 32
DP = 8
ZN = 8
GROUP = 4
TILE = 128
EVENTS = 64
CH = 24
D = SEQ * CH
BINS = SEQ * TILE
COLS = 3 * CH
LANES = CH * TILE
f32 = jnp.float32
bf16 = jnp.bfloat16
MESH = pl.DeviceIdType.MESH
VMEM = pl.BlockSpec(memory_space=pltpu.VMEM)
SMEM = pl.BlockSpec(memory_space=pltpu.SMEM)
ANY = pl.BlockSpec(memory_space=pl.ANY)
LIMIT = 48 * 1024 * 1024


def tables():
    a = np.arange(SEQ)
    j = np.arange(TILE)
    k1 = np.arange(SEQ) + 0.25
    k2 = np.arange(TILE)
    first = np.exp(-2j * np.pi * np.outer(k1, a) / SEQ)
    turn = np.exp(-2j * np.pi * np.outer(k1, j) / BINS)
    second = np.exp(-2j * np.pi * np.outer(j, k2) / TILE)
    w1 = np.concatenate([first.real, first.imag], axis=0)
    w2 = np.block([[second.real, second.imag], [-second.imag, second.real]])
    inv2 = np.conj(second).T
    v2 = np.block([[inv2.real, inv2.imag], [-inv2.imag, inv2.real]])
    last = np.conj(first).T / BINS
    v1 = np.concatenate([last.real, -last.imag], axis=1)
    tw = np.stack([turn.real, turn.imag])

    def split(t):
        t = t.astype(np.float32)
        hi = t.astype(jnp.bfloat16)
        lo = (t - hi.astype(np.float32)).astype(jnp.bfloat16)
        return hi, lo

    w1h, w1l = split(w1)
    w2h, w2l = split(w2)
    v2h, v2l = split(v2)
    v1h, v1l = split(v1)
    return (
        np.concatenate([w1h, w1l], axis=1),
        np.concatenate([w2h, w2h, w2l], axis=0),
        np.concatenate([v2h, v2h, v2l], axis=0),
        np.concatenate([v1h, v1h, v1l], axis=1),
        tw.astype(np.float32),
    )


def dot(x, y):
    return jnp.dot(x, y, preferred_element_type=f32)


def split(x):
    hi = x.astype(bf16)
    lo = (x - hi.astype(f32)).astype(bf16)
    return hi, lo


def rnd(x):
    return x.astype(bf16).astype(f32)


def compute_kernel(
    lev_ref, wt_ref, b1_ref, b2_ref, cot_ref, f1_ref, f2_ref,
    w1_ref, w2_ref, v2_ref, v1_ref, tw_ref,
    out_ref, gf_ref, gw_ref,
    levs, rows, crows, val, g1, g2, hid, gm, m1, m2, gh,
    tmp, inv, hat1, hat2, hatv, hath, hatg, gpb,
):
    scale = 1.0 / math.sqrt(DP * BINS)
    base = lax.axis_index("seq") * CH

    def lanes(c):
        return slice(c * TILE, (c + 1) * TILE)

    def krows(c):
        return slice(c * SEQ, (c + 1) * SEQ)

    def put3(c, re, im):
        rh, rl = split(re)
        ih, il = split(im)
        tmp[krows(c), 0:128] = rh
        tmp[krows(c), 128:256] = ih
        tmp[krows(c), 256:384] = rl
        tmp[krows(c), 384:512] = il
        tmp[krows(c), 512:640] = rh
        tmp[krows(c), 640:768] = ih

    def forward(x_ref, dst):
        cr = tw_ref[0]
        ci = tw_ref[1]
        for p in range(CH // 2):
            x = x_ref[:, p * 256:(p + 1) * 256]
            part = dot(w1_ref[...], jnp.concatenate([x, x], axis=0))
            for h in range(2):
                re = part[0:32, lanes(h)]
                im = part[32:64, lanes(h)]
                put3(2 * p + h, re * cr - im * ci, re * ci + im * cr)
        dst[...] = dot(tmp[...], w2_ref[...])

    def inverse(left, right, conj, emit):
        cr = tw_ref[0]
        ci = tw_ref[1]
        for c in range(CH):
            lr = left[krows(c), 0:128]
            li = left[krows(c), 128:256]
            rr = right[krows(c), 0:128]
            ri = right[krows(c), 128:256]
            if conj:
                put3(c, lr * rr + li * ri, lr * ri - li * rr)
            else:
                put3(c, lr * rr - li * ri, lr * ri + li * rr)
        inv[...] = dot(tmp[...], v2_ref[...])
        for p in range(CH // 2):
            cols = []
            for h in range(2):
                c = 2 * p + h
                re = inv[krows(c), 0:128]
                im = inv[krows(c), 128:256]
                rh, rl = split(re * cr + im * ci)
                ih, il = split(im * cr - re * ci)
                cols.append(jnp.concatenate([rh, ih, rl, il, rh, ih], axis=0))
            res = dot(v1_ref[...], jnp.concatenate(cols, axis=1))
            for h in range(2):
                emit(2 * p + h, res[:, lanes(h)])

    for a in range(SEQ):
        levs[0:EVENTS, a * TILE:(a + 1) * TILE] = lev_ref[a % GROUP, a // GROUP]
    levs[EVENTS:, :] = jnp.zeros((TILE - EVENTS, BINS), bf16)
    for p in range(SEQ // 2):
        proj = dot(wt_ref[...], levs[0:EVENTS, p * 256:(p + 1) * 256])
        for h in range(2):
            a = 2 * p + h
            rows[a * COLS:(a + 1) * COLS, :] = proj[:, lanes(h)]
    for c in range(CH):
        val[:, lanes(c)] = rows[pl.ds(c, SEQ, stride=COLS), :].astype(bf16)
        g1[:, lanes(c)] = rows[pl.ds(CH + c, SEQ, stride=COLS), :].astype(bf16)
        g2[:, lanes(c)] = rows[pl.ds(2 * CH + c, SEQ, stride=COLS), :].astype(bf16)

    def load_filter(ref, dst):
        for d in range(DP):
            for q in range(BINS // DP // TILE):
                a = d * (BINS // DP // TILE) + q
                crows[a * CH:(a + 1) * CH, :] = ref[d, :, q * TILE:(q + 1) * TILE].astype(f32)
        for c in range(CH):
            hid[:, lanes(c)] = crows[pl.ds(c, SEQ, stride=CH), :].astype(bf16)
        forward(hid, dst)

    load_filter(f1_ref, hat1)
    load_filter(f2_ref, hat2)

    forward(val, hatv)

    def emit_one(c, conv):
        mixed = rnd(conv) + b1_ref[base + c] * val[:, lanes(c)].astype(f32)
        m1[:, lanes(c)] = mixed
        hid[:, lanes(c)] = (g1[:, lanes(c)].astype(f32) * mixed).astype(bf16)

    inverse(hat1, hatv, False, emit_one)
    forward(hid, hath)

    for a in range(SEQ):
        crows[a * CH:(a + 1) * CH, :] = cot_ref[a].astype(f32)

    def emit_two(c, conv):
        mixed = rnd(conv) + b2_ref[base + c] * hid[:, lanes(c)].astype(f32)
        up = crows[pl.ds(c, SEQ, stride=CH), :] * scale
        gate = g2[:, lanes(c)].astype(f32)
        rows[pl.ds(2 * CH + c, SEQ, stride=COLS), :] = up * mixed
        m2[:, lanes(c)] = gate * mixed
        gm[:, lanes(c)] = (up * gate).astype(bf16)

    inverse(hat2, hath, False, emit_two)
    for c in range(CH):
        crows[pl.ds(c, SEQ, stride=CH), :] = m2[:, lanes(c)]
    for a in range(SEQ):
        out_ref[a] = crows[a * CH:(a + 1) * CH, :].astype(bf16)

    forward(gm, hatg)
    bias_rows = []
    for c in range(CH):
        s = gm[:, lanes(c)].astype(f32) * hid[:, lanes(c)].astype(f32)
        bias_rows.append(jnp.sum(s, axis=0, keepdims=True))
    sum_two = jnp.sum(jnp.concatenate(bias_rows, axis=0), axis=1, keepdims=True)

    def emit_carried_two(c, conv):
        ghid = b2_ref[base + c] * gm[:, lanes(c)].astype(f32) + rnd(conv)
        gh[:, lanes(c)] = (ghid * g1[:, lanes(c)].astype(f32)).astype(bf16)
        rows[pl.ds(CH + c, SEQ, stride=COLS), :] = ghid * m1[:, lanes(c)]

    inverse(hat2, hatg, True, emit_carried_two)

    def emit_gf(which):
        def emit(c, conv):
            gf_ref[c // 3, which, :, (c % 3) * TILE:(c % 3 + 1) * TILE] = conv.astype(bf16)
        return emit

    inverse(hath, hatg, True, emit_gf(1))
    forward(gh, hatg)
    bias_rows = []
    for c in range(CH):
        s = gh[:, lanes(c)].astype(f32) * val[:, lanes(c)].astype(f32)
        bias_rows.append(jnp.sum(s, axis=0, keepdims=True))
    sum_one = jnp.sum(jnp.concatenate(bias_rows, axis=0), axis=1, keepdims=True)

    def emit_carried_one(c, conv):
        rows[pl.ds(c, SEQ, stride=COLS), :] = (
            b1_ref[base + c] * gh[:, lanes(c)].astype(f32) + rnd(conv)
        )

    inverse(hat1, hatg, True, emit_carried_one)
    inverse(hatv, hatg, True, emit_gf(0))
    for a in range(SEQ):
        gpb[:, a * TILE:(a + 1) * TILE] = rows[a * COLS:(a + 1) * COLS, :].astype(bf16)
    weight = lax.dot_general(
        gpb[...], levs[...], (((1,), (1,)), ((), ())), preferred_element_type=f32
    )
    sums = jnp.concatenate([sum_one, sum_two, jnp.zeros((CH, 1), f32)], axis=0)
    lane = lax.broadcasted_iota(jnp.int32, (COLS, TILE), 1)
    gw_ref[...] = weight + jnp.where(lane == EVENTS, sums, 0.0)


def compute(lev, wt, b1, b2, cot, f1, f2):
    w1, w2, v2, v1, tw = tables()
    return pl.pallas_call(
        compute_kernel,
        out_shape=(
            jax.ShapeDtypeStruct((SEQ, CH, TILE), bf16),
            jax.ShapeDtypeStruct((DP, 2, SEQ, 3 * TILE), bf16),
            jax.ShapeDtypeStruct((COLS, TILE), f32),
        ),
        in_specs=[VMEM, VMEM, SMEM, SMEM] + [VMEM] * 8,
        out_specs=(VMEM, VMEM, VMEM),
        scratch_shapes=[
            pltpu.VMEM((TILE, BINS), bf16),
            pltpu.VMEM((SEQ * COLS, TILE), f32),
            pltpu.VMEM((SEQ * CH, TILE), f32),
            pltpu.VMEM((SEQ, LANES), bf16),
            pltpu.VMEM((SEQ, LANES), bf16),
            pltpu.VMEM((SEQ, LANES), bf16),
            pltpu.VMEM((SEQ, LANES), bf16),
            pltpu.VMEM((SEQ, LANES), bf16),
            pltpu.VMEM((SEQ, LANES), f32),
            pltpu.VMEM((SEQ, LANES), f32),
            pltpu.VMEM((SEQ, LANES), bf16),
            pltpu.VMEM((SEQ * CH, 6 * TILE), bf16),
            pltpu.VMEM((SEQ * CH, 2 * TILE), f32),
            pltpu.VMEM((SEQ * CH, 2 * TILE), f32),
            pltpu.VMEM((SEQ * CH, 2 * TILE), f32),
            pltpu.VMEM((SEQ * CH, 2 * TILE), f32),
            pltpu.VMEM((SEQ * CH, 2 * TILE), f32),
            pltpu.VMEM((SEQ * CH, 2 * TILE), f32),
            pltpu.VMEM((COLS, BINS), bf16),
        ],
        compiler_params=pltpu.CompilerParams(vmem_limit_bytes=LIMIT),
        name="transforms",
    )(lev, wt, b1, b2, cot, f1, f2, w1, w2, v2, v1, tw)


def place():
    s = lax.axis_index("seq")
    d = lax.axis_index("dp")
    return s, d, s // GROUP, lax.rem(s, GROUP)


def seq_peer(s, i):
    return {"seq": lax.rem(s + i, SEQ)}


def dp_peer(d, i):
    return {"dp": lax.rem(d + i, DP)}


def z_peer(z, q, i):
    return {"seq": lax.rem(z + i, ZN) * GROUP + q}


def q_peer(z, q, r):
    return {"seq": z * GROUP + lax.rem(q + r, GROUP)}


def push(src, dst, send, recv, device):
    return pltpu.make_async_remote_copy(
        src_ref=src, dst_ref=dst, send_sem=send, recv_sem=recv,
        device_id=device, device_id_type=MESH,
    )


def greet(s, d):
    barrier = pltpu.get_barrier_semaphore()

    def hello_seq(i, _):
        pl.semaphore_signal(barrier, inc=1, device_id=seq_peer(s, i), device_id_type=MESH)
        return 0

    def hello_dp(i, _):
        pl.semaphore_signal(barrier, inc=1, device_id=dp_peer(d, i), device_id_type=MESH)
        return 0

    lax.fori_loop(1, SEQ, hello_seq, 0)
    lax.fori_loop(1, DP, hello_dp, 0)
    return lambda: pl.semaphore_wait(barrier, SEQ + DP - 2)


def each(low, high, f):
    def step(i, _):
        f(i)
        return 0

    lax.fori_loop(low, high, step, 0)


def entry_kernel(
    counts_ref, w_ref, cot_ref, f1_ref, f2_ref,
    lev_ref, wt_ref, cotg_ref, fg1_ref, fg2_ref,
    own, wtt, loc, zs, zr, gs, gr, fs, fr, cs, cr,
):
    s, d, z, q = place()
    wait_barrier = greet(s, d)
    levels = jnp.log1p(counts_ref[...].astype(f32)) - 3.0
    own[...] = levels.T.astype(bf16)
    wait_barrier()

    def z_copy(i):
        return push(own, lev_ref.at[q, z], zs.at[i], zr.at[i], z_peer(z, q, i))

    def g_copy(r, i):
        slot = lev_ref.at[q, lax.rem(z - i + ZN, ZN)]
        return push(slot, slot, gs.at[r, i], gr.at[r, i], q_peer(z, q, r))

    def f_copy(i, src, dst, k):
        return push(src, dst.at[d], fs.at[k, i], fr.at[k, i], dp_peer(d, i))

    def c_copy(i):
        return push(
            cot_ref.at[lax.rem(s + i, SEQ)], cotg_ref.at[s], cs.at[i], cr.at[i], seq_peer(s, i)
        )

    each(1, ZN, lambda i: z_copy(i).start())
    keep = pltpu.make_async_copy(own, lev_ref.at[q, z], loc.at[0])
    keep.start()
    keep_cot = pltpu.make_async_copy(cot_ref.at[s], cotg_ref.at[s], loc.at[1])
    keep_cot.start()
    keep_f1 = pltpu.make_async_copy(f1_ref, fg1_ref.at[d], loc.at[2])
    keep_f1.start()
    keep_f2 = pltpu.make_async_copy(f2_ref, fg2_ref.at[d], loc.at[3])
    keep_f2.start()

    def send_filters(i):
        f_copy(i, f1_ref, fg1_ref, 0).start()
        f_copy(i, f2_ref, fg2_ref, 1).start()

    each(1, DP, send_filters)
    each(1, SEQ, lambda i: c_copy(i).start())
    keep.wait()
    for r in range(1, GROUP):
        g_copy(r, 0).start()
    wtt[...] = w_ref[...].astype(f32).T
    for k in range(3):
        at = pl.multiple_of(k * D + s * CH, 8)
        wt_ref[k * CH:(k + 1) * CH, :] = wtt[pl.ds(at, CH), :].astype(bf16)

    def pass_on(i):
        z_copy(i).wait_recv()
        for r in range(1, GROUP):
            g_copy(r, i).start()

    each(1, ZN, pass_on)
    keep_cot.wait()
    keep_f1.wait()
    keep_f2.wait()
    each(1, ZN, lambda i: z_copy(i).wait_send())

    def end_filters(i):
        f_copy(i, f1_ref, fg1_ref, 0).wait()
        f_copy(i, f2_ref, fg2_ref, 1).wait()

    each(1, DP, end_filters)
    each(1, SEQ, lambda i: c_copy(i).wait())

    def end_group(i):
        for r in range(1, GROUP):
            g_copy(r, i).wait()

    each(0, ZN, end_group)


def entry(counts, w_in, cot, f1, f2):
    dma = pltpu.SemaphoreType.DMA
    return pl.pallas_call(
        entry_kernel,
        out_shape=(
            jax.ShapeDtypeStruct((GROUP, ZN, EVENTS, TILE), bf16),
            jax.ShapeDtypeStruct((COLS, EVENTS), bf16),
            jax.ShapeDtypeStruct((SEQ, CH, TILE), bf16),
            jax.ShapeDtypeStruct((DP, CH, BINS // DP), bf16),
            jax.ShapeDtypeStruct((DP, CH, BINS // DP), bf16),
        ),
        in_specs=[VMEM, VMEM, ANY, ANY, ANY],
        out_specs=(ANY, VMEM, ANY, ANY, ANY),
        scratch_shapes=[
            pltpu.VMEM((EVENTS, TILE), bf16),
            pltpu.VMEM((3 * D, EVENTS), f32),
            dma((4,)),
            dma((ZN,)),
            dma((ZN,)),
            dma((GROUP, ZN)),
            dma((GROUP, ZN)),
            dma((2, DP)),
            dma((2, DP)),
            dma((SEQ,)),
            dma((SEQ,)),
        ],
        compiler_params=pltpu.CompilerParams(
            collective_id=0, has_side_effects=True, vmem_limit_bytes=LIMIT
        ),
        name="entry",
    )(counts, w_in, cot, f1, f2)


def exit_kernel(
    out_ref, gf_ref, gw_ref,
    outg_ref, gf1_ref, gf2_ref, gwo_ref, gb_ref,
    gf_all, gw_in, gw_all, flat, loc, zs, zr, gs, gr, fs, fr, ws, wr, cs, cr,
):
    s, d, z, q = place()
    greet(s, d)()

    def w_copy(i):
        return push(gw_ref, gw_in.at[d], ws.at[i], wr.at[i], dp_peer(d, i))

    def f_copy(i):
        to = lax.rem(d + i, DP)
        return push(gf_ref.at[to], gf_all.at[d], fs.at[i], fr.at[i], dp_peer(d, i))

    def c_copy(i):
        return push(
            out_ref.at[lax.rem(s + i, SEQ)], outg_ref.at[s], cs.at[i], cr.at[i], seq_peer(s, i)
        )

    def z_copy(i):
        slot = gw_all.at[:, s]
        return push(slot, slot, zs.at[i], zr.at[i], z_peer(z, q, i))

    def g_copy(r, i):
        slot = gw_all.at[:, lax.rem(z - i + ZN, ZN) * GROUP + q]
        return push(slot, slot, gs.at[r, i], gr.at[r, i], q_peer(z, q, r))

    each(1, DP, lambda i: w_copy(i).start())
    keep_gw = pltpu.make_async_copy(gw_ref, gw_in.at[d], loc.at[0])
    keep_gw.start()
    each(1, DP, lambda i: f_copy(i).start())
    keep_gf = pltpu.make_async_copy(gf_ref.at[d], gf_all.at[d], loc.at[1])
    keep_gf.start()
    each(1, SEQ, lambda i: c_copy(i).start())
    keep_out = pltpu.make_async_copy(out_ref.at[s], outg_ref.at[s], loc.at[2])
    keep_out.start()
    keep_gw.wait()
    each(1, DP, lambda i: w_copy(i).wait())
    total = gw_in[0]
    for k in range(1, DP):
        total = total + gw_in[k]
    for k in range(3):
        gw_all[k, s] = total[k * CH:(k + 1) * CH]
    each(1, ZN, lambda i: z_copy(i).start())
    for r in range(1, GROUP):
        g_copy(r, 0).start()

    keep_gf.wait()
    each(1, DP, lambda i: f_copy(i).wait())

    def pass_on(i):
        z_copy(i).wait_recv()
        for r in range(1, GROUP):
            g_copy(r, i).start()

    each(1, ZN, pass_on)

    for which, dst in ((0, gf1_ref), (1, gf2_ref)):
        total = gf_all[0, which].astype(f32)
        for k in range(1, DP):
            total = total + gf_all[k, which].astype(f32)
        for c in range(3):
            for a in range(SEQ):
                flat[c:c + 1, a * TILE:(a + 1) * TILE] = total[
                    a:a + 1, c * TILE:(c + 1) * TILE
                ]
        dst[...] = flat[0:3, :].astype(bf16)

    each(1, ZN, lambda i: z_copy(i).wait_send())

    def end_group(i):
        for r in range(1, GROUP):
            g_copy(r, i).wait()

    each(0, ZN, end_group)
    for k in range(3):
        block = gw_all[k].reshape(D, TILE)
        for p in range(D // TILE):
            turned = block[p * TILE:(p + 1) * TILE, :].T
            at = k * D + p * TILE
            gwo_ref[:, at:at + TILE] = turned[0:EVENTS, :]
            if k < 2:
                gb_ref[k:k + 1, p * TILE:(p + 1) * TILE] = turned[EVENTS:EVENTS + 1, :]
    keep_out.wait()
    each(1, SEQ, lambda i: c_copy(i).wait())


def leave(out, gf, gw):
    dma = pltpu.SemaphoreType.DMA
    return pl.pallas_call(
        exit_kernel,
        out_shape=(
            jax.ShapeDtypeStruct((SEQ, CH, TILE), bf16),
            jax.ShapeDtypeStruct((3, BINS), bf16),
            jax.ShapeDtypeStruct((3, BINS), bf16),
            jax.ShapeDtypeStruct((EVENTS, 3 * D), f32),
            jax.ShapeDtypeStruct((2, D), f32),
        ),
        in_specs=[ANY, ANY, ANY],
        out_specs=(ANY, VMEM, VMEM, VMEM, VMEM),
        scratch_shapes=[
            pltpu.VMEM((DP, 2, SEQ, 3 * TILE), bf16),
            pltpu.VMEM((DP, COLS, TILE), f32),
            pltpu.VMEM((3, SEQ, CH, TILE), f32),
            pltpu.VMEM((8, BINS), f32),
            dma((3,)),
            dma((ZN,)),
            dma((ZN,)),
            dma((GROUP, ZN)),
            dma((GROUP, ZN)),
            dma((DP,)),
            dma((DP,)),
            dma((DP,)),
            dma((DP,)),
            dma((SEQ,)),
            dma((SEQ,)),
        ],
        compiler_params=pltpu.CompilerParams(
            collective_id=1, has_side_effects=True, vmem_limit_bytes=LIMIT
        ),
        name="leave",
    )(out, gf, gw)


def body(counts, w_in, bias_one, bias_two, filter_one, filter_two, cotangent):
    lev, wt, cot, f1, f2 = entry(
        counts[0], w_in, cotangent.reshape(SEQ, CH, TILE), filter_one, filter_two
    )
    out, gf, gw = compute(lev, wt, bias_one, bias_two, cot, f1, f2)
    out, gf1, gf2, gw, gb = leave(out, gf, gw)
    return out.reshape(1, D, TILE), gw, gb[0], gb[1], gf1, gf2


def solution(mesh):
    return jax.shard_map(
        body,
        mesh=mesh,
        in_specs=(
            P("dp", "seq", None),
            P(),
            P(),
            P(),
            P("seq", "dp"),
            P("seq", "dp"),
            P("dp", None, "seq"),
        ),
        out_specs=(
            P("dp", None, "seq"),
            P(),
            P(),
            P(),
            P(("seq", "dp"), None),
            P(("seq", "dp"), None),
        ),
        check_vma=False,
    )
```

```python
import functools
import math

import jax
import jax.numpy as jnp
import numpy as np
from jax import lax
from jax.experimental import pallas as pl
from jax.experimental.pallas import tpu as pltpu
from jax.sharding import PartitionSpec as P

SEQ = 32
DP = 8
ZN = 8
GROUP = 4
TILE = 128
EVENTS = 64
CH = 24
D = SEQ * CH
BINS = SEQ * TILE
COLS = 3 * CH
LANES = CH * TILE
f32 = jnp.float32
bf16 = jnp.bfloat16
MESH = pl.DeviceIdType.MESH
VMEM = pl.BlockSpec(memory_space=pltpu.VMEM)
SMEM = pl.BlockSpec(memory_space=pltpu.SMEM)
ANY = pl.BlockSpec(memory_space=pl.ANY)
LIMIT = 56 * 1024 * 1024


def tables():
    a = np.arange(SEQ)
    j = np.arange(TILE)
    k1 = np.arange(SEQ) + 0.25
    k2 = np.arange(TILE)
    first = np.exp(-2j * np.pi * np.outer(k1, a) / SEQ)
    turn = np.exp(-2j * np.pi * np.outer(k1, j) / BINS)
    second = np.exp(-2j * np.pi * np.outer(j, k2) / TILE)
    w1 = np.concatenate([first.real, first.imag], axis=0)
    w2 = np.block([[second.real, second.imag], [-second.imag, second.real]])
    inv2 = np.conj(second).T
    v2 = np.block([[inv2.real, inv2.imag], [-inv2.imag, inv2.real]])
    last = np.conj(first).T / BINS
    v1 = np.concatenate([last.real, -last.imag], axis=1)

    table = np.zeros((640, 2 * TILE), np.float32)
    table[0:256] = w2
    table[256:512] = v2
    table[512:576, 0:32] = w1
    table[576:608, 0:64] = v1
    table[608:640, 0:128] = turn.real
    table[608:640, 128:256] = turn.imag
    return table


def dot(x, y):
    return jnp.dot(x, y, preferred_element_type=f32)


def split(x):
    hi = x.astype(bf16)
    lo = (x - hi.astype(f32)).astype(bf16)
    return hi, lo


def rnd(x):
    return x.astype(bf16).astype(f32)


def place():
    s = lax.axis_index("seq")
    d = lax.axis_index("dp")
    return s, d, s // GROUP, lax.rem(s, GROUP)


def seq_peer(s, i):
    return {"seq": lax.rem(s + i, SEQ)}


def dp_peer(d, i):
    return {"dp": lax.rem(d + i, DP)}


def z_peer(z, q, i):
    return {"seq": lax.rem(z + i, ZN) * GROUP + q}


def q_peer(z, q, r):
    return {"seq": z * GROUP + lax.rem(q + r, GROUP)}


def push(src, dst, send, recv, device):
    return pltpu.make_async_remote_copy(
        src_ref=src, dst_ref=dst, send_sem=send, recv_sem=recv,
        device_id=device, device_id_type=MESH,
    )


def greet(s, d):
    barrier = pltpu.get_barrier_semaphore()

    def hello_seq(i, _):
        pl.semaphore_signal(barrier, inc=1, device_id=seq_peer(s, i), device_id_type=MESH)
        return 0

    def hello_dp(i, _):
        pl.semaphore_signal(barrier, inc=1, device_id=dp_peer(d, i), device_id_type=MESH)
        return 0

    lax.fori_loop(1, SEQ, hello_seq, 0)
    lax.fori_loop(1, DP, hello_dp, 0)
    return lambda: pl.semaphore_wait(barrier, SEQ + DP - 2)


def each(low, high, f):
    def step(i, _):
        f(i)
        return 0

    lax.fori_loop(low, high, step, 0)


def whole_kernel(
    counts_in, w_in, b1_ref, b2_ref, cot_in, f1_in, f2_in,
    table_in,
    outg_ref, gf1_ref, gf2_ref, gwo_ref, gb_ref,
    counts_ref, w_ref, table, w1_ref, w2_ref, v2_ref, v1_ref, tw_ref,
    own, wtt, wt_ref, lev_ref, cot_ref, f1_ref, f2_ref,
    levs, rows, crows, val, g1, g2, hid, gm, m1, m2, gh,
    tmp, inv, hat1, hat2, hatv, hath, hatg, gpb,
    out_s, gf_s, gwp, gf_all, gw_in, gw_all, flat,
    pre, loc, zs, zr, gs, gr, fs, fr, cs, cr,
    os_, or_, hs, hr, ks, kr, azs, azr, ags, agr, vs, vr,
):
    s, d, z, q = place()
    wait_barrier = greet(s, d)
    loads = [
        pltpu.make_async_copy(a, b, pre.at[i])
        for i, (a, b) in enumerate((
            (counts_in, counts_ref), (w_in, w_ref), (table_in, table),
        ))
    ]
    for load in loads:
        load.start()
    scale = 1.0 / math.sqrt(DP * BINS)
    base = s * CH

    def lanes(c):
        return slice(c * TILE, (c + 1) * TILE)

    def krows(c):
        return slice(c * SEQ, (c + 1) * SEQ)

    def put3(c, re, im):
        rh, rl = split(re)
        ih, il = split(im)
        tmp[krows(c), 0:128] = rh
        tmp[krows(c), 128:256] = ih
        tmp[krows(c), 256:384] = rl
        tmp[krows(c), 384:512] = il
        tmp[krows(c), 512:640] = rh
        tmp[krows(c), 640:768] = ih

    def forward(x_ref, dst):
        cr_ = tw_ref[0]
        ci_ = tw_ref[1]
        for p in range(CH // 2):
            x = x_ref[:, p * 256:(p + 1) * 256]
            part = dot(w1_ref[...], jnp.concatenate([x, x], axis=0))
            for h in range(2):
                re = part[0:32, lanes(h)]
                im = part[32:64, lanes(h)]
                put3(2 * p + h, re * cr_ - im * ci_, re * ci_ + im * cr_)
        dst[...] = dot(tmp[...], w2_ref[...])

    def inverse(left, right, conj, emit):
        cr_ = tw_ref[0]
        ci_ = tw_ref[1]
        for c in range(CH):
            lr = left[krows(c), 0:128]
            li = left[krows(c), 128:256]
            rr = right[krows(c), 0:128]
            ri = right[krows(c), 128:256]
            if conj:
                put3(c, lr * rr + li * ri, lr * ri - li * rr)
            else:
                put3(c, lr * rr - li * ri, lr * ri + li * rr)
        inv[...] = dot(tmp[...], v2_ref[...])
        for p in range(CH // 2):
            cols = []
            for h in range(2):
                c = 2 * p + h
                re = inv[krows(c), 0:128]
                im = inv[krows(c), 128:256]
                rh, rl = split(re * cr_ + im * ci_)
                ih, il = split(im * cr_ - re * ci_)
                cols.append(jnp.concatenate([rh, ih, rl, il, rh, ih], axis=0))
            res = dot(v1_ref[...], jnp.concatenate(cols, axis=1))
            for h in range(2):
                emit(2 * p + h, res[:, lanes(h)])

    def z_copy(i):
        return push(own, lev_ref.at[q, z], zs.at[i], zr.at[i], z_peer(z, q, i))

    def g_copy(r, i):
        slot = lev_ref.at[q, lax.rem(z - i + ZN, ZN)]
        return push(slot, slot, gs.at[r, i], gr.at[r, i], q_peer(z, q, r))

    def f_copy(i, src, dst, k):
        return push(src, dst.at[d], fs.at[k, i], fr.at[k, i], dp_peer(d, i))

    def c_copy(i):
        return push(
            cot_in.at[lax.rem(s + i, SEQ)], cot_ref.at[s], cs.at[i], cr.at[i], seq_peer(s, i)
        )

    def o_copy(i):
        return push(
            out_s.at[lax.rem(s + i, SEQ)], outg_ref.at[s], os_.at[i], or_.at[i], seq_peer(s, i)
        )

    def h_copy(which, i):
        to = lax.rem(d + i, DP)
        return push(
            gf_s.at[which, to], gf_all.at[which, d], hs.at[which, i], hr.at[which, i],
            dp_peer(d, i),
        )

    def k_copy(part, i):
        at = slice(0, CH) if part == 0 else slice(CH, COLS)
        return push(
            gwp.at[at], gw_in.at[d, at], ks.at[part, i], kr.at[part, i], dp_peer(d, i)
        )

    def az_copy(i):
        slot = gw_all.at[1:3, s]
        return push(slot, slot, azs.at[i], azr.at[i], z_peer(z, q, i))

    def ag_copy(r, i):
        slot = gw_all.at[1:3, lax.rem(z - i + ZN, ZN) * GROUP + q]
        return push(slot, slot, ags.at[r, i], agr.at[r, i], q_peer(z, q, r))

    def v_copy(i):
        slot = gw_all.at[0, s]
        return push(slot, slot, vs.at[i], vr.at[i], seq_peer(s, i))

    loads[0].wait()
    levels = jnp.log1p(counts_ref[...].astype(f32)) - 3.0
    own[...] = levels.astype(bf16)
    lev_ref[q, z] = own[...]
    wait_barrier()
    each(1, ZN, lambda i: z_copy(i).start())

    def send_filters(i):
        f_copy(i, f1_in, f1_ref, 0).start()
        f_copy(i, f2_in, f2_ref, 1).start()

    each(1, DP, send_filters)
    for r in range(1, GROUP):
        g_copy(r, 0).start()
    each(1, SEQ, lambda i: c_copy(i).start())
    keeps = [
        pltpu.make_async_copy(f1_in, f1_ref.at[d], loc.at[0]),
        pltpu.make_async_copy(f2_in, f2_ref.at[d], loc.at[1]),
        pltpu.make_async_copy(cot_in.at[s], cot_ref.at[s], loc.at[2]),
    ]
    for keep in keeps:
        keep.start()
    loads[1].wait()
    wtt[...] = w_ref[...].astype(f32).T
    for k in range(3):
        at = pl.multiple_of(k * D + s * CH, 8)
        wt_ref[k * CH:(k + 1) * CH, :] = wtt[pl.ds(at, CH), :].astype(bf16)
    levs[EVENTS:, :] = jnp.zeros((TILE - EVENTS, BINS), bf16)
    loads[2].wait()
    for at, ref in ((0, w2_ref), (256, v2_ref)):
        hi, lo = split(table[at:at + 256, :])
        ref[0:256, :] = hi
        ref[256:512, :] = hi
        ref[512:768, :] = lo
    hi, lo = split(table[512:576, 0:32])
    w1_ref[...] = jnp.concatenate([hi, lo], axis=1)
    hi, lo = split(table[576:608, 0:64])
    v1_ref[...] = jnp.concatenate([hi, hi, lo], axis=1)
    tw_ref[0] = table[608:640, 0:128]
    tw_ref[1] = table[608:640, 128:256]

    def pass_on(i):
        z_copy(i).wait_recv()
        for r in range(1, GROUP):
            g_copy(r, i).start()

    each(1, ZN, pass_on)

    def load_filter(ref, dst):
        for e in range(DP):
            for p in range(BINS // DP // TILE):
                a = e * (BINS // DP // TILE) + p
                crows[a * CH:(a + 1) * CH, :] = ref[e, :, p * TILE:(p + 1) * TILE].astype(f32)
        for c in range(CH):
            hid[:, lanes(c)] = crows[pl.ds(c, SEQ, stride=CH), :].astype(bf16)
        forward(hid, dst)

    keeps[0].wait()
    each(1, DP, lambda i: f_copy(i, f1_in, f1_ref, 0).wait())
    load_filter(f1_ref, hat1)
    keeps[1].wait()
    each(1, DP, lambda i: f_copy(i, f2_in, f2_ref, 1).wait())
    load_filter(f2_ref, hat2)

    each(1, ZN, lambda i: z_copy(i).wait_send())

    def end_group(i):
        for r in range(1, GROUP):
            g_copy(r, i).wait()

    each(0, ZN, end_group)
    for a in range(SEQ):
        levs[0:EVENTS, a * TILE:(a + 1) * TILE] = lev_ref[a % GROUP, a // GROUP]
    for p in range(SEQ // 2):
        proj = dot(wt_ref[...], levs[0:EVENTS, p * 256:(p + 1) * 256])
        for h in range(2):
            a = 2 * p + h
            rows[a * COLS:(a + 1) * COLS, :] = proj[:, lanes(h)]
    for c in range(CH):
        val[:, lanes(c)] = rows[pl.ds(c, SEQ, stride=COLS), :].astype(bf16)
        g1[:, lanes(c)] = rows[pl.ds(CH + c, SEQ, stride=COLS), :].astype(bf16)
        g2[:, lanes(c)] = rows[pl.ds(2 * CH + c, SEQ, stride=COLS), :].astype(bf16)
    forward(val, hatv)

    def emit_one(c, conv):
        mixed = rnd(conv) + b1_ref[base + c] * val[:, lanes(c)].astype(f32)
        m1[:, lanes(c)] = mixed
        hid[:, lanes(c)] = (g1[:, lanes(c)].astype(f32) * mixed).astype(bf16)

    inverse(hat1, hatv, False, emit_one)
    forward(hid, hath)

    keeps[2].wait()
    each(1, SEQ, lambda i: c_copy(i).wait())
    for a in range(SEQ):
        crows[a * CH:(a + 1) * CH, :] = cot_ref[a].astype(f32)

    def emit_two(c, conv):
        mixed = rnd(conv) + b2_ref[base + c] * hid[:, lanes(c)].astype(f32)
        up = crows[pl.ds(c, SEQ, stride=CH), :] * scale
        gate = g2[:, lanes(c)].astype(f32)
        rows[pl.ds(2 * CH + c, SEQ, stride=COLS), :] = up * mixed
        m2[:, lanes(c)] = gate * mixed
        gm[:, lanes(c)] = (up * gate).astype(bf16)

    inverse(hat2, hath, False, emit_two)
    for c in range(CH):
        crows[pl.ds(c, SEQ, stride=CH), :] = m2[:, lanes(c)]
    for a in range(SEQ):
        out_s[a] = crows[a * CH:(a + 1) * CH, :].astype(bf16)
    each(1, SEQ, lambda i: o_copy(i).start())
    keep_out = pltpu.make_async_copy(out_s.at[s], outg_ref.at[s], loc.at[3])
    keep_out.start()

    def bias_sums(x_ref, y_ref):
        parts = []
        for c in range(CH):
            t = x_ref[:, lanes(c)].astype(f32) * y_ref[:, lanes(c)].astype(f32)
            parts.append(jnp.sum(t, axis=0, keepdims=True))
        return jnp.sum(jnp.concatenate(parts, axis=0), axis=1, keepdims=True)

    def weight_rows(low, high, sums):
        for a in range(SEQ):
            gpb[low:high, a * TILE:(a + 1) * TILE] = rows[
                a * COLS + low:a * COLS + high, :
            ].astype(bf16)
        weight = lax.dot_general(
            gpb[low:high, :], levs[...], (((1,), (1,)), ((), ())), preferred_element_type=f32
        )
        lane = lax.broadcasted_iota(jnp.int32, (high - low, TILE), 1)
        gwp[low:high, :] = weight + jnp.where(lane == EVENTS, sums, 0.0)
        gw_in[d, low:high, :] = gwp[low:high, :]

    def total_rows(low, high):
        total = gw_in[0, low:high, :]
        for k in range(1, DP):
            total = total + gw_in[k, low:high, :]
        for k in range(low // CH, high // CH):
            gw_all[k, s] = total[k * CH - low:(k + 1) * CH - low].astype(bf16)

    def emit_gf(which):
        def emit(c, conv):
            gf_s[which, c // 3, :, (c % 3) * TILE:(c % 3 + 1) * TILE] = conv.astype(bf16)
        return emit

    def finish_filter(which, dst):
        each(1, DP, lambda i: h_copy(which, i).wait())
        total = gf_all[which, 0].astype(f32)
        for k in range(1, DP):
            total = total + gf_all[which, k].astype(f32)
        for c in range(3):
            for a in range(SEQ):
                flat[c:c + 1, a * TILE:(a + 1) * TILE] = total[a:a + 1, lanes(c)]
        dst[...] = flat[0:3, :].astype(bf16)

    forward(gm, hatg)
    sum_two = bias_sums(gm, hid)

    def emit_carried_two(c, conv):
        ghid = b2_ref[base + c] * gm[:, lanes(c)].astype(f32) + rnd(conv)
        gh[:, lanes(c)] = (ghid * g1[:, lanes(c)].astype(f32)).astype(bf16)
        rows[pl.ds(CH + c, SEQ, stride=COLS), :] = ghid * m1[:, lanes(c)]

    inverse(hat2, hatg, True, emit_carried_two)
    weight_rows(CH, COLS, jnp.concatenate([sum_two, jnp.zeros((CH, 1), f32)], axis=0))
    each(1, DP, lambda i: k_copy(1, i).start())

    inverse(hath, hatg, True, emit_gf(1))
    gf_all[1, d] = gf_s[1, d]
    each(1, DP, lambda i: h_copy(1, i).start())

    forward(gh, hatg)
    sum_one = bias_sums(gh, val)

    def emit_carried_one(c, conv):
        rows[pl.ds(c, SEQ, stride=COLS), :] = (
            b1_ref[base + c] * gh[:, lanes(c)].astype(f32) + rnd(conv)
        )

    inverse(hat1, hatg, True, emit_carried_one)
    weight_rows(0, CH, sum_one)
    each(1, DP, lambda i: k_copy(0, i).start())

    each(1, DP, lambda i: k_copy(1, i).wait())
    total_rows(CH, COLS)
    each(1, ZN, lambda i: az_copy(i).start())
    for r in range(1, GROUP):
        ag_copy(r, 0).start()

    inverse(hatv, hatg, True, emit_gf(0))
    gf_all[0, d] = gf_s[0, d]
    each(1, DP, lambda i: h_copy(0, i).start())

    each(1, DP, lambda i: k_copy(0, i).wait())
    total_rows(0, CH)
    each(1, SEQ, lambda i: v_copy(i).start())

    def pass_on_weights(i):
        az_copy(i).wait_recv()
        for r in range(1, GROUP):
            ag_copy(r, i).start()

    each(1, ZN, pass_on_weights)
    finish_filter(1, gf2_ref)
    finish_filter(0, gf1_ref)
    each(1, ZN, lambda i: az_copy(i).wait_send())

    def end_weights(i):
        for r in range(1, GROUP):
            ag_copy(r, i).wait()

    def turn(k):
        block = gw_all[k].astype(f32).reshape(D, TILE)
        for p in range(D // TILE):
            turned = block[p * TILE:(p + 1) * TILE, :].T
            at = k * D + p * TILE
            gwo_ref[:, at:at + TILE] = turned[0:EVENTS, :]
            if k < 2:
                gb_ref[k:k + 1, p * TILE:(p + 1) * TILE] = turned[EVENTS:EVENTS + 1, :]

    each(0, ZN, end_weights)
    turn(1)
    turn(2)
    each(1, SEQ, lambda i: v_copy(i).wait())
    turn(0)
    keep_out.wait()
    each(1, SEQ, lambda i: o_copy(i).wait())


def whole(counts, w_in, b1, b2, cot, f1, f2):
    dma = pltpu.SemaphoreType.DMA
    vm = pltpu.VMEM
    spec = (SEQ * CH, 2 * TILE)
    return pl.pallas_call(
        whole_kernel,
        out_shape=(
            jax.ShapeDtypeStruct((SEQ, CH, TILE), bf16),
            jax.ShapeDtypeStruct((3, BINS), bf16),
            jax.ShapeDtypeStruct((3, BINS), bf16),
            jax.ShapeDtypeStruct((EVENTS, 3 * D), f32),
            jax.ShapeDtypeStruct((2, D), f32),
        ),
        in_specs=[ANY, ANY, SMEM, SMEM] + [ANY] * 4,
        out_specs=(ANY, VMEM, VMEM, VMEM, VMEM),
        scratch_shapes=[
            vm((EVENTS, TILE), jnp.int32),
            vm((EVENTS, 3 * D), bf16),
            vm((640, 2 * TILE), f32),
            vm((2 * SEQ, 2 * SEQ), bf16),
            vm((6 * TILE, 2 * TILE), bf16),
            vm((6 * TILE, 2 * TILE), bf16),
            vm((SEQ, 6 * SEQ), bf16),
            vm((2, SEQ, TILE), f32),
            vm((EVENTS, TILE), bf16),
            vm((3 * D, EVENTS), f32),
            vm((COLS, EVENTS), bf16),
            vm((GROUP, ZN, EVENTS, TILE), bf16),
            vm((SEQ, CH, TILE), bf16),
            vm((DP, CH, BINS // DP), bf16),
            vm((DP, CH, BINS // DP), bf16),
            vm((TILE, BINS), bf16),
            vm((SEQ * COLS, TILE), f32),
            vm((SEQ * CH, TILE), f32),
            vm((SEQ, LANES), bf16),
            vm((SEQ, LANES), bf16),
            vm((SEQ, LANES), bf16),
            vm((SEQ, LANES), bf16),
            vm((SEQ, LANES), bf16),
            vm((SEQ, LANES), f32),
            vm((SEQ, LANES), f32),
            vm((SEQ, LANES), bf16),
            vm((SEQ * CH, 6 * TILE), bf16),
            vm(spec, f32),
            vm(spec, f32),
            vm(spec, f32),
            vm(spec, f32),
            vm(spec, f32),
            vm(spec, f32),
            vm((COLS, BINS), bf16),
            vm((SEQ, CH, TILE), bf16),
            vm((2, DP, SEQ, 3 * TILE), bf16),
            vm((COLS, TILE), f32),
            vm((2, DP, SEQ, 3 * TILE), bf16),
            vm((DP, COLS, TILE), f32),
            vm((3, SEQ, CH, TILE), bf16),
            vm((8, BINS), f32),
            dma((3,)),
            dma((4,)),
            dma((ZN,)),
            dma((ZN,)),
            dma((GROUP, ZN)),
            dma((GROUP, ZN)),
            dma((2, DP)),
            dma((2, DP)),
            dma((SEQ,)),
            dma((SEQ,)),
            dma((SEQ,)),
            dma((SEQ,)),
            dma((2, DP)),
            dma((2, DP)),
            dma((2, DP)),
            dma((2, DP)),
            dma((ZN,)),
            dma((ZN,)),
            dma((GROUP, ZN)),
            dma((GROUP, ZN)),
            dma((SEQ,)),
            dma((SEQ,)),
        ],
        compiler_params=pltpu.CompilerParams(
            collective_id=0, has_side_effects=True, vmem_limit_bytes=LIMIT
        ),
        name="whole",
    )(counts, w_in, b1, b2, cot, f1, f2, tables())


def body(counts, w_in, bias_one, bias_two, filter_one, filter_two, cotangent):
    out, gf1, gf2, gw, gb = whole(
        counts[0].T, w_in, bias_one, bias_two, cotangent.reshape(SEQ, CH, TILE),
        filter_one, filter_two,
    )
    return out.reshape(1, D, TILE), gw, gb[0], gb[1], gf1, gf2


def solution(mesh):
    return jax.shard_map(
        body,
        mesh=mesh,
        in_specs=(
            P("dp", "seq", None),
            P(),
            P(),
            P(),
            P("seq", "dp"),
            P("seq", "dp"),
            P("dp", None, "seq"),
        ),
        out_specs=(
            P("dp", None, "seq"),
            P(),
            P(),
            P(),
            P(("seq", "dp"), None),
            P(("seq", "dp"), None),
        ),
        check_vma=False,
    )
```

```python
import functools
import math

import jax
import jax.numpy as jnp
import numpy as np
from jax import lax
from jax.experimental import pallas as pl
from jax.experimental.pallas import tpu as pltpu
from jax.sharding import PartitionSpec as P

SEQ = 32
DP = 8
ZN = 8
GROUP = 4
TILE = 128
EVENTS = 64
CH = 24
D = SEQ * CH
BINS = SEQ * TILE
COLS = 3 * CH
LANES = CH * TILE
f32 = jnp.float32
bf16 = jnp.bfloat16
MESH = pl.DeviceIdType.MESH
VMEM = pl.BlockSpec(memory_space=pltpu.VMEM)
SMEM = pl.BlockSpec(memory_space=pltpu.SMEM)
ANY = pl.BlockSpec(memory_space=pl.ANY)
LIMIT = 56 * 1024 * 1024


def tables():
    a = np.arange(SEQ)
    j = np.arange(TILE)
    k1 = np.arange(SEQ) + 0.25
    k2 = np.arange(TILE)
    first = np.exp(-2j * np.pi * np.outer(k1, a) / SEQ)
    turn = np.exp(-2j * np.pi * np.outer(k1, j) / BINS)
    second = np.exp(-2j * np.pi * np.outer(j, k2) / TILE)
    w1 = np.concatenate([first.real, first.imag], axis=0)
    w2 = np.block([[second.real, second.imag], [-second.imag, second.real]])
    inv2 = np.conj(second).T
    v2 = np.block([[inv2.real, inv2.imag], [-inv2.imag, inv2.real]])
    last = np.conj(first).T / BINS
    v1 = np.concatenate([last.real, -last.imag], axis=1)

    table = np.zeros((640, 2 * TILE), np.float32)
    table[0:256] = w2
    table[256:512] = v2
    table[512:576, 0:32] = w1
    table[576:608, 0:64] = v1
    table[608:640, 0:128] = turn.real
    table[608:640, 128:256] = turn.imag
    return table


def dot(x, y):
    return jnp.dot(x, y, preferred_element_type=f32)


def split(x):
    hi = x.astype(bf16)
    lo = (x - hi.astype(f32)).astype(bf16)
    return hi, lo


def rnd(x):
    return x.astype(bf16).astype(f32)


def place():
    s = lax.axis_index("seq")
    d = lax.axis_index("dp")
    return s, d, s // GROUP, lax.rem(s, GROUP)


def dp_peer(d, i):
    return {"dp": lax.rem(d + i, DP)}


def z_peer(z, q, i):
    return {"seq": lax.rem(z + i, ZN) * GROUP + q}


def q_peer(z, q, r):
    return {"seq": z * GROUP + lax.rem(q + r, GROUP)}


def push(src, dst, send, recv, device):
    return pltpu.make_async_remote_copy(
        src_ref=src, dst_ref=dst, send_sem=send, recv_sem=recv,
        device_id=device, device_id_type=MESH,
    )


def greet(z, q, d):
    barrier = pltpu.get_barrier_semaphore()

    def hello(device):
        pl.semaphore_signal(barrier, inc=1, device_id=device, device_id_type=MESH)

    for i in range(1, ZN):
        hello(z_peer(z, q, i))
    for i in range(1, GROUP):
        hello(q_peer(z, q, i))
    for i in range(1, DP):
        hello(dp_peer(d, i))
    return lambda: pl.semaphore_wait(barrier, ZN + GROUP + DP - 3)


def received(ref, sem, device):
    push(ref, ref, sem, sem, device).wait_recv()


def sent(ref, sem, device):
    push(ref, ref, sem, sem, device).wait_send()


def each(low, high, f):
    def step(i, _):
        f(i)
        return 0

    lax.fori_loop(low, high, step, 0)


def whole_kernel(
    counts_in, w_in, b1_in, b2_in, cot_in, f1_in, f2_in, table_in,
    outg_ref, gf1_ref, gf2_ref, gwo_ref, gb_ref,
    counts_ref, w_ref, table, b1_ref, b2_ref, w1_ref, w2_ref, v2_ref, v1_ref, tw_ref,
    own, wtt, wt_ref, lev_ref, cot_mid, cot_ref, f1_ref, f2_ref,
    levs, rows, crows, val, g1, g2, hid, gm, m1, m2, gh,
    tmp, inv, hat1, hat2, hatv, hath, hatg, hat_one_grad, gpb,
    out_s, out_mid, gf_s, gwp, gf_all, gw_in, gw_all, flat, gf_o, gw_o, gb_o,
    pre, loc, done, zr, zs, gs, gr, fs, fr, cs, cr, os_, or_, hs, hr, ks, kr, ws, wr,
):
    s, d, z, q = place()
    wait_barrier = greet(z, q, d)
    friend = dp_peer(d, 1)
    loads = [
        pltpu.make_async_copy(a, b, pre.at[i])
        for i, (a, b) in enumerate((
            (counts_in, counts_ref), (w_in, w_ref), (table_in, table),
            (b1_in, b1_ref), (b2_in, b2_ref),
        ))
    ]
    for load in loads:
        load.start()
    scale = 1.0 / math.sqrt(DP * BINS)
    base = s * CH

    def lanes(c):
        return slice(c * TILE, (c + 1) * TILE)

    def krows(c):
        return slice(c * SEQ, (c + 1) * SEQ)

    def put3(c, re, im):
        rh, rl = split(re)
        ih, il = split(im)
        tmp[krows(c), 0:128] = rh
        tmp[krows(c), 128:256] = ih
        tmp[krows(c), 256:384] = rl
        tmp[krows(c), 384:512] = il
        tmp[krows(c), 512:640] = rh
        tmp[krows(c), 640:768] = ih

    def forward(x_ref, dst):
        cr_ = tw_ref[0]
        ci_ = tw_ref[1]
        for p in range(CH // 2):
            x = x_ref[:, p * 256:(p + 1) * 256]
            part = dot(w1_ref[...], jnp.concatenate([x, x], axis=0))
            for h in range(2):
                re = part[0:32, lanes(h)]
                im = part[32:64, lanes(h)]
                put3(2 * p + h, re * cr_ - im * ci_, re * ci_ + im * cr_)
        dst[...] = dot(tmp[...], w2_ref[...])

    def inverse(left, right, conj, emit):
        cr_ = tw_ref[0]
        ci_ = tw_ref[1]
        for c in range(CH):
            lr = left[krows(c), 0:128]
            li = left[krows(c), 128:256]
            rr = right[krows(c), 0:128]
            ri = right[krows(c), 128:256]
            if conj:
                put3(c, lr * rr + li * ri, lr * ri - li * rr)
            else:
                put3(c, lr * rr - li * ri, lr * ri + li * rr)
        inv[...] = dot(tmp[...], v2_ref[...])
        for p in range(CH // 2):
            cols = []
            for h in range(2):
                c = 2 * p + h
                re = inv[krows(c), 0:128]
                im = inv[krows(c), 128:256]
                rh, rl = split(re * cr_ + im * ci_)
                ih, il = split(im * cr_ - re * ci_)
                cols.append(jnp.concatenate([rh, ih, rl, il, rh, ih], axis=0))
            res = dot(v1_ref[...], jnp.concatenate(cols, axis=1))
            for h in range(2):
                emit(2 * p + h, res[:, lanes(h)])

    def z_copy(i):
        return push(own, lev_ref.at[q, z], zs.at[0], zr.at[i], z_peer(z, q, i))

    def g_copy(r, i):
        slot = lev_ref.at[q, lax.rem(z - i + ZN, ZN)]
        return push(slot, slot, gs.at[0], gr.at[0], q_peer(z, q, r))

    def f_copy(i, src, dst, k):
        return push(src, dst.at[d], fs.at[k], fr.at[k], dp_peer(d, i))

    def line_copy(i, src, mid, k, send, recv):
        to = lax.rem(z + i, ZN)
        return push(src.at[to], mid.at[z], send.at[k], recv.at[k], z_peer(z, q, i))

    def plane_copy(r, mid, dst, k, send, recv):
        to = lax.rem(q + r, GROUP)
        return push(mid.at[:, to], dst.at[:, q], send.at[k], recv.at[k], q_peer(z, q, r))

    def h_copy(which, i):
        to = lax.rem(d + i, DP)
        return push(
            gf_s.at[which, to], gf_all.at[which, d], hs.at[which], hr.at[which], dp_peer(d, i)
        )

    def part_rows(part):
        return slice(0, CH) if part == 0 else slice(CH, COLS)

    def k_copy(part, i):
        at = part_rows(part)
        return push(gwp.at[at], gw_in.at[d, at], ks.at[part], kr.at[part], dp_peer(d, i))

    def part_blocks(part):
        return slice(0, 1) if part == 0 else slice(1, 3)

    def wz_copy(part, i):
        slot = gw_all.at[part_blocks(part), z, q]
        return push(slot, slot, ws.at[part], wr.at[part], z_peer(z, q, i))

    def wg_copy(part, r):
        slot = gw_all.at[part_blocks(part), :, q]
        return push(slot, slot, ws.at[2 + part], wr.at[2 + part], q_peer(z, q, r))

    loads[0].wait()
    levels = jnp.log1p(counts_ref[...].astype(f32)) - 3.0
    own[...] = levels.astype(bf16)
    lev_ref[q, z] = own[...]
    wait_barrier()
    each(1, ZN, lambda i: z_copy(i).start())

    def send_filters(i):
        f_copy(i, f1_in, f1_ref, 0).start()
        f_copy(i, f2_in, f2_ref, 1).start()

    each(1, DP, send_filters)
    for r in range(1, GROUP):
        g_copy(r, 0).start()
    keeps = [
        pltpu.make_async_copy(f1_in, f1_ref.at[d], loc.at[0]),
        pltpu.make_async_copy(f2_in, f2_ref.at[d], loc.at[1]),
        pltpu.make_async_copy(cot_in.at[z], cot_mid.at[z], loc.at[2]),
    ]
    for keep in keeps:
        keep.start()
    loads[1].wait()
    wtt[...] = w_ref[...].astype(f32).T
    for k in range(3):
        at = pl.multiple_of(k * D + s * CH, 8)
        wt_ref[k * CH:(k + 1) * CH, :] = wtt[pl.ds(at, CH), :].astype(bf16)
    levs[EVENTS:, :] = jnp.zeros((TILE - EVENTS, BINS), bf16)
    for load in loads[2:]:
        load.wait()
    for at, ref in ((0, w2_ref), (256, v2_ref)):
        hi, lo = split(table[at:at + 256, :])
        ref[0:256, :] = hi
        ref[256:512, :] = hi
        ref[512:768, :] = lo
    hi, lo = split(table[512:576, 0:32])
    w1_ref[...] = jnp.concatenate([hi, lo], axis=1)
    hi, lo = split(table[576:608, 0:64])
    v1_ref[...] = jnp.concatenate([hi, hi, lo], axis=1)
    tw_ref[0] = table[608:640, 0:128]
    tw_ref[1] = table[608:640, 128:256]

    for i in (1, 7, 2, 6, 3, 5, 4):
        z_copy(i).wait_recv()
        for r in range(1, GROUP):
            g_copy(r, i).start()
    for i in range(1, ZN):
        line_copy(i, cot_in, cot_mid, 0, cs, cr).start()

    def load_filter(ref, dst):
        for e in range(DP):
            for p in range(BINS // DP // TILE):
                a = e * (BINS // DP // TILE) + p
                crows[a * CH:(a + 1) * CH, :] = ref[e, :, p * TILE:(p + 1) * TILE].astype(f32)
        for c in range(CH):
            hid[:, lanes(c)] = crows[pl.ds(c, SEQ, stride=CH), :].astype(bf16)
        forward(hid, dst)

    keeps[0].wait()
    received(f1_ref.at[0:DP - 1], fr.at[0], friend)
    load_filter(f1_ref, hat1)
    keeps[1].wait()
    received(f2_ref.at[0:DP - 1], fr.at[1], friend)
    load_filter(f2_ref, hat2)

    received(lev_ref.at[0:GROUP - 1], gr.at[0], friend)
    for a in range(SEQ):
        levs[0:EVENTS, a * TILE:(a + 1) * TILE] = lev_ref[a % GROUP, a // GROUP]
    for p in range(SEQ // 2):
        proj = dot(wt_ref[...], levs[0:EVENTS, p * 256:(p + 1) * 256])
        for h in range(2):
            a = 2 * p + h
            rows[a * COLS:(a + 1) * COLS, :] = proj[:, lanes(h)]
    for c in range(CH):
        val[:, lanes(c)] = rows[pl.ds(c, SEQ, stride=COLS), :].astype(bf16)
        g1[:, lanes(c)] = rows[pl.ds(CH + c, SEQ, stride=COLS), :].astype(bf16)
        g2[:, lanes(c)] = rows[pl.ds(2 * CH + c, SEQ, stride=COLS), :].astype(bf16)
    keeps[2].wait()
    received(cot_mid.at[0:ZN - 1], cr.at[0], friend)
    for r in range(1, GROUP):
        plane_copy(r, cot_mid, cot_ref, 1, cs, cr).start()
    keep_cot = pltpu.make_async_copy(cot_mid.at[:, q], cot_ref.at[:, q], loc.at[3])
    keep_cot.start()
    forward(val, hatv)

    def emit_one(c, conv):
        mixed = rnd(conv) + b1_ref[base + c] * val[:, lanes(c)].astype(f32)
        m1[:, lanes(c)] = mixed
        hid[:, lanes(c)] = (g1[:, lanes(c)].astype(f32) * mixed).astype(bf16)

    inverse(hat1, hatv, False, emit_one)
    forward(hid, hath)

    keep_cot.wait()
    received(cot_ref.at[:, 0:GROUP - 1], cr.at[1], friend)
    for a in range(SEQ):
        crows[a * CH:(a + 1) * CH, :] = cot_ref[a // GROUP, a % GROUP].astype(f32)

    def emit_two(c, conv):
        mixed = rnd(conv) + b2_ref[base + c] * hid[:, lanes(c)].astype(f32)
        up = crows[pl.ds(c, SEQ, stride=CH), :] * scale
        gate = g2[:, lanes(c)].astype(f32)
        rows[pl.ds(2 * CH + c, SEQ, stride=COLS), :] = up * mixed
        m2[:, lanes(c)] = gate * mixed
        gm[:, lanes(c)] = (up * gate).astype(bf16)

    inverse(hat2, hath, False, emit_two)
    for c in range(CH):
        crows[pl.ds(c, SEQ, stride=CH), :] = m2[:, lanes(c)]
    for a in range(SEQ):
        out_s[a // GROUP, a % GROUP] = crows[a * CH:(a + 1) * CH, :].astype(bf16)
    for i in range(1, ZN):
        line_copy(i, out_s, out_mid, 0, os_, or_).start()
    keep_out = pltpu.make_async_copy(out_s.at[z], out_mid.at[z], loc.at[4])
    keep_out.start()

    def bias_sums(x_ref, y_ref):
        parts = []
        for c in range(CH):
            t = x_ref[:, lanes(c)].astype(f32) * y_ref[:, lanes(c)].astype(f32)
            parts.append(jnp.sum(t, axis=0, keepdims=True))
        return jnp.sum(jnp.concatenate(parts, axis=0), axis=1, keepdims=True)

    def weight_rows(low, high, sums):
        for a in range(SEQ):
            gpb[low:high, a * TILE:(a + 1) * TILE] = rows[
                a * COLS + low:a * COLS + high, :
            ].astype(bf16)
        weight = lax.dot_general(
            gpb[low:high, :], levs[...], (((1,), (1,)), ((), ())), preferred_element_type=f32
        )
        lane = lax.broadcasted_iota(jnp.int32, (high - low, TILE), 1)
        gwp[low:high, :] = weight + jnp.where(lane == EVENTS, sums, 0.0)
        gw_in[d, low:high, :] = gwp[low:high, :]

    def total_rows(low, high):
        total = gw_in[0, low:high, :]
        for k in range(1, DP):
            total = total + gw_in[k, low:high, :]
        for k in range(low // CH, high // CH):
            gw_all[k, z, q] = total[k * CH - low:(k + 1) * CH - low].astype(bf16)

    def emit_gf(which):
        def emit(c, conv):
            gf_s[which, c // 3, :, (c % 3) * TILE:(c % 3 + 1) * TILE] = conv.astype(bf16)
        return emit

    gives = []

    def give(src, dst, k):
        copy = pltpu.make_async_copy(src, dst, done.at[k])
        copy.start()
        gives.append(copy)

    def finish_filter(which, dst):
        received(gf_all.at[which, 0:DP - 1], hr.at[which], friend)
        total = gf_all[which, 0].astype(f32)
        for k in range(1, DP):
            total = total + gf_all[which, k].astype(f32)
        for c in range(3):
            for a in range(SEQ):
                flat[c:c + 1, a * TILE:(a + 1) * TILE] = total[a:a + 1, lanes(c)]
        gf_o[which] = flat[0:3, :].astype(bf16)
        give(gf_o.at[which], dst, which)

    forward(gm, hatg)
    sum_two = bias_sums(gm, hid)

    def emit_carried_two(c, conv):
        ghid = b2_ref[base + c] * gm[:, lanes(c)].astype(f32) + rnd(conv)
        gh[:, lanes(c)] = (ghid * g1[:, lanes(c)].astype(f32)).astype(bf16)
        rows[pl.ds(CH + c, SEQ, stride=COLS), :] = ghid * m1[:, lanes(c)]

    inverse(hat2, hatg, True, emit_carried_two)
    weight_rows(CH, COLS, jnp.concatenate([sum_two, jnp.zeros((CH, 1), f32)], axis=0))
    for i in range(1, DP):
        k_copy(1, i).start()

    forward(gh, hat_one_grad)
    sum_one = bias_sums(gh, val)

    def emit_carried_one(c, conv):
        rows[pl.ds(c, SEQ, stride=COLS), :] = (
            b1_ref[base + c] * gh[:, lanes(c)].astype(f32) + rnd(conv)
        )

    inverse(hat1, hat_one_grad, True, emit_carried_one)
    weight_rows(0, CH, sum_one)
    for i in range(1, DP):
        k_copy(0, i).start()

    inverse(hath, hatg, True, emit_gf(1))
    gf_all[1, d] = gf_s[1, d]
    for i in range(1, DP):
        h_copy(1, i).start()

    received(gw_in.at[0:DP - 1, part_rows(1)], kr.at[1], friend)
    total_rows(CH, COLS)
    for i in range(1, ZN):
        wz_copy(1, i).start()
    keep_out.wait()
    received(out_mid.at[0:ZN - 1], or_.at[0], friend)
    for r in range(1, GROUP):
        plane_copy(r, out_mid, outg_ref, 1, os_, or_).start()
    keep_plane = pltpu.make_async_copy(out_mid.at[:, q], outg_ref.at[:, q], loc.at[5])
    keep_plane.start()

    inverse(hatv, hat_one_grad, True, emit_gf(0))
    gf_all[0, d] = gf_s[0, d]
    for i in range(1, DP):
        h_copy(0, i).start()

    received(gw_in.at[0:DP - 1, part_rows(0)], kr.at[0], friend)
    total_rows(0, CH)
    for i in range(1, ZN):
        wz_copy(0, i).start()

    def turn(k):
        block = gw_all[k].astype(f32).reshape(D, TILE)
        for p in range(D // TILE):
            turned = block[p * TILE:(p + 1) * TILE, :].T
            at = k * D + p * TILE
            gw_o[:, at:at + TILE] = turned[0:EVENTS, :]
            if k < 2:
                gb_o[k:k + 1, p * TILE:(p + 1) * TILE] = turned[EVENTS:EVENTS + 1, :]
        at = slice(k * D, (k + 1) * D)
        give(gw_o.at[:, at], gwo_ref.at[:, at], 2 + k)

    def pass_weights(part):
        received(gw_all.at[part_blocks(part), 0:ZN - 1, 0], wr.at[part], friend)
        for r in range(1, GROUP):
            wg_copy(part, r).start()

    pass_weights(1)
    finish_filter(1, gf2_ref)
    pass_weights(0)
    finish_filter(0, gf1_ref)
    received(gw_all.at[part_blocks(1), :, 0:GROUP - 1], wr.at[3], friend)
    turn(1)
    turn(2)
    received(gw_all.at[part_blocks(0), :, 0:GROUP - 1], wr.at[2], friend)
    turn(0)
    give(gb_o, gb_ref, 5)
    keep_plane.wait()
    received(outg_ref.at[:, 0:GROUP - 1], or_.at[1], friend)
    sent(lev_ref.at[0, 0:ZN - 1], zs.at[0], friend)
    sent(lev_ref.at[0:GROUP - 1], gs.at[0], friend)
    sent(f1_ref.at[0:DP - 1], fs.at[0], friend)
    sent(f2_ref.at[0:DP - 1], fs.at[1], friend)
    sent(cot_mid.at[0:ZN - 1], cs.at[0], friend)
    sent(cot_ref.at[:, 0:GROUP - 1], cs.at[1], friend)
    sent(out_mid.at[0:ZN - 1], os_.at[0], friend)
    sent(outg_ref.at[:, 0:GROUP - 1], os_.at[1], friend)
    for part in range(2):
        sent(gf_all.at[part, 0:DP - 1], hs.at[part], friend)
        sent(gw_in.at[0:DP - 1, part_rows(part)], ks.at[part], friend)
        sent(gw_all.at[part_blocks(part), 0:ZN - 1, 0], ws.at[part], friend)
        sent(gw_all.at[part_blocks(part), :, 0:GROUP - 1], ws.at[2 + part], friend)
    for copy in gives:
        copy.wait()


def whole(counts, w_in, b1, b2, cot, f1, f2):
    dma = pltpu.SemaphoreType.DMA
    vm = pltpu.VMEM
    spec = (SEQ * CH, 2 * TILE)
    return pl.pallas_call(
        whole_kernel,
        out_shape=(
            jax.ShapeDtypeStruct((ZN, GROUP, CH, TILE), bf16),
            jax.ShapeDtypeStruct((3, BINS), bf16),
            jax.ShapeDtypeStruct((3, BINS), bf16),
            jax.ShapeDtypeStruct((EVENTS, 3 * D), f32),
            jax.ShapeDtypeStruct((2, D), f32),
        ),
        in_specs=[ANY] * 8,
        out_specs=(ANY,) * 5,
        scratch_shapes=[
            vm((EVENTS, TILE), jnp.int32),
            vm((EVENTS, 3 * D), bf16),
            vm((640, 2 * TILE), f32),
            pltpu.SMEM((D,), f32),
            pltpu.SMEM((D,), f32),
            vm((2 * SEQ, 2 * SEQ), bf16),
            vm((6 * TILE, 2 * TILE), bf16),
            vm((6 * TILE, 2 * TILE), bf16),
            vm((SEQ, 6 * SEQ), bf16),
            vm((2, SEQ, TILE), f32),
            vm((EVENTS, TILE), bf16),
            vm((3 * D, EVENTS), f32),
            vm((COLS, EVENTS), bf16),
            vm((GROUP, ZN, EVENTS, TILE), bf16),
            vm((ZN, GROUP, CH, TILE), bf16),
            vm((ZN, GROUP, CH, TILE), bf16),
            vm((DP, CH, BINS // DP), bf16),
            vm((DP, CH, BINS // DP), bf16),
            vm((TILE, BINS), bf16),
            vm((SEQ * COLS, TILE), f32),
            vm((SEQ * CH, TILE), f32),
            vm((SEQ, LANES), bf16),
            vm((SEQ, LANES), bf16),
            vm((SEQ, LANES), bf16),
            vm((SEQ, LANES), bf16),
            vm((SEQ, LANES), bf16),
            vm((SEQ, LANES), f32),
            vm((SEQ, LANES), f32),
            vm((SEQ, LANES), bf16),
            vm((SEQ * CH, 6 * TILE), bf16),
            vm(spec, f32),
            vm(spec, f32),
            vm(spec, f32),
            vm(spec, f32),
            vm(spec, f32),
            vm(spec, f32),
            vm(spec, f32),
            vm((COLS, BINS), bf16),
            vm((ZN, GROUP, CH, TILE), bf16),
            vm((ZN, GROUP, CH, TILE), bf16),
            vm((2, DP, SEQ, 3 * TILE), bf16),
            vm((COLS, TILE), f32),
            vm((2, DP, SEQ, 3 * TILE), bf16),
            vm((DP, COLS, TILE), f32),
            vm((3, ZN, GROUP, CH, TILE), bf16),
            vm((8, BINS), f32),
            vm((2, 3, BINS), bf16),
            vm((EVENTS, 3 * D), f32),
            vm((2, D), f32),
            dma((5,)),
            dma((6,)),
            dma((6,)),
            dma((8,)),
            dma((1,)),
            dma((1,)),
            dma((1,)),
            dma((2,)),
            dma((2,)),
            dma((2,)),
            dma((2,)),
            dma((2,)),
            dma((2,)),
            dma((2,)),
            dma((2,)),
            dma((2,)),
            dma((2,)),
            dma((4,)),
            dma((4,)),
        ],
        compiler_params=pltpu.CompilerParams(
            collective_id=0, has_side_effects=True, vmem_limit_bytes=LIMIT
        ),
        name="whole",
    )(counts, w_in, b1, b2, cot, f1, f2, tables())


def finish_kernel(
    out_in, gf1_in, gf2_in, gw_in, gb_in, out_ref, gf1_ref, gf2_ref, gw_ref, gb1_ref, gb2_ref
):
    out_ref[...] = out_in[...]
    gf1_ref[...] = gf1_in[...]
    gf2_ref[...] = gf2_in[...]
    gw_ref[...] = gw_in[...]
    gb1_ref[...] = gb_in[0]
    gb2_ref[...] = gb_in[1]


def finish(out, gf1, gf2, gw, gb):
    like = [jax.ShapeDtypeStruct(x.shape, x.dtype) for x in (out, gf1, gf2, gw)]
    flat = jax.ShapeDtypeStruct((D,), f32)
    return pl.pallas_call(
        finish_kernel,
        out_shape=(*like, flat, flat),
        in_specs=[VMEM] * 5,
        out_specs=(VMEM,) * 6,
        compiler_params=pltpu.CompilerParams(vmem_limit_bytes=LIMIT),
        name="finish",
    )(out, gf1, gf2, gw, gb)


def body(counts, w_in, bias_one, bias_two, filter_one, filter_two, cotangent):
    out, gf1, gf2, gw, gb = whole(
        counts[0].T, w_in, bias_one, bias_two, cotangent.reshape(ZN, GROUP, CH, TILE),
        filter_one, filter_two,
    )
    out, gf1, gf2, gw, gb1, gb2 = finish(out.reshape(1, D, TILE), gf1, gf2, gw, gb)
    return out, gw, gb1, gb2, gf1, gf2


def solution(mesh):
    return jax.shard_map(
        body,
        mesh=mesh,
        in_specs=(
            P("dp", "seq", None),
            P(),
            P(),
            P(),
            P("seq", "dp"),
            P("seq", "dp"),
            P("dp", None, "seq"),
        ),
        out_specs=(
            P("dp", None, "seq"),
            P(),
            P(),
            P(),
            P(("seq", "dp"), None),
            P(("seq", "dp"), None),
        ),
        check_vma=False,
    )
```

```python
import functools
import math

import jax
import jax.numpy as jnp
import numpy as np
from jax import lax
from jax.experimental import pallas as pl
from jax.experimental.pallas import tpu as pltpu
from jax.sharding import PartitionSpec as P

SEQ = 32
DP = 8
ZN = 8
GROUP = 4
TILE = 128
EVENTS = 64
CH = 24
D = SEQ * CH
BINS = SEQ * TILE
COLS = 3 * CH
LANES = CH * TILE
f32 = jnp.float32
bf16 = jnp.bfloat16
MESH = pl.DeviceIdType.MESH
VMEM = pl.BlockSpec(memory_space=pltpu.VMEM)
SMEM = pl.BlockSpec(memory_space=pltpu.SMEM)
ANY = pl.BlockSpec(memory_space=pl.ANY)
LIMIT = 56 * 1024 * 1024
LINE = (4, 3, 5, 2, 6, 1, 7)
FAR = (8, 7, 9, 6, 10, 5, 11, 4, 12, 3, 13, 2, 14, 1, 15)


def tables():
    a = np.arange(SEQ)
    j = np.arange(TILE)
    k1 = np.arange(SEQ) + 0.25
    k2 = np.arange(TILE)
    first = np.exp(-2j * np.pi * np.outer(k1, a) / SEQ)
    turn = np.exp(-2j * np.pi * np.outer(k1, j) / BINS)
    second = np.exp(-2j * np.pi * np.outer(j, k2) / TILE)
    w1 = np.concatenate([first.real, first.imag], axis=0)
    w2 = np.block([[second.real, second.imag], [-second.imag, second.real]])
    inv2 = np.conj(second).T
    v2 = np.block([[inv2.real, inv2.imag], [-inv2.imag, inv2.real]])
    last = np.conj(first).T / BINS
    v1 = np.concatenate([last.real, -last.imag], axis=1)

    table = np.zeros((640, 2 * TILE), np.float32)
    table[0:256] = w2
    table[256:512] = v2
    table[512:576, 0:32] = w1
    table[576:608, 0:64] = v1
    table[608:640, 0:128] = turn.real
    table[608:640, 128:256] = turn.imag
    return table


def dot(x, y):
    return jnp.dot(x, y, preferred_element_type=f32)


def split(x):
    hi = x.astype(bf16)
    lo = (x - hi.astype(f32)).astype(bf16)
    return hi, lo


def rnd(x):
    return x.astype(bf16).astype(f32)


def place():
    s = lax.axis_index("seq")
    d = lax.axis_index("dp")
    return s, d, s // GROUP, lax.rem(s, GROUP)


def dp_peer(d, i):
    return {"dp": lax.rem(d + i, DP)}


def z_peer(z, q, i):
    return {"seq": lax.rem(z + i, ZN) * GROUP + q}


def q_peer(z, q, r):
    return {"seq": z * GROUP + lax.rem(q + r, GROUP)}


def push(src, dst, send, recv, device):
    return pltpu.make_async_remote_copy(
        src_ref=src, dst_ref=dst, send_sem=send, recv_sem=recv,
        device_id=device, device_id_type=MESH,
    )


def same_core(s, i):
    return {"seq": lax.rem(s + 2 * i, SEQ)}


def core_peer(s):
    return {"seq": s + 1 - 2 * lax.rem(s, 2)}


def pair(d):
    return d + 1 - 2 * lax.rem(d, 2)


def greet(s, z, q, d):
    barrier = pltpu.get_barrier_semaphore()

    def hello(device):
        pl.semaphore_signal(barrier, inc=1, device_id=device, device_id_type=MESH)

    for i in range(1, SEQ // 2):
        hello(same_core(s, i))
    hello(core_peer(s))
    for i in range(1, DP):
        hello(dp_peer(d, i))
    return lambda: pl.semaphore_wait(barrier, SEQ // 2 + DP - 1)


def received(ref, sem, device):
    push(ref, ref, sem, sem, device).wait_recv()


def sent(ref, sem, device):
    push(ref, ref, sem, sem, device).wait_send()


def each(low, high, f):
    def step(i, _):
        f(i)
        return 0

    lax.fori_loop(low, high, step, 0)


def whole_kernel(
    counts_in, w_in, b1_in, b2_in, cot_in, f1_in, f2_in, table_in,
    outg_ref, gf1_ref, gf2_ref, gwo_ref, gb_ref,
    counts_ref, w_ref, table, b1_ref, b2_ref, w1_ref, w2_ref, v2_ref, v1_ref, tw_ref,
    own, wtt, wt_ref, lev_ref, cot_mid, cot_ref, f1_ref, f2_ref,
    levs, rows, crows, val, g1, g2, hid, gm, m1, m2, gh,
    tmp, inv, hat1, hat2, hatv, hath, hatg, hat_one_grad, gpb,
    out_s, out_mid, gf_s, gwp, gf_all, gw_in, gw_v, gw_g, flat, gf_o, gw_o, gb_o,
    pre, loc, done, zr, xr, zs, gs, gr, fs, fr, cs, cr, os_, or_, hs, hr, ks, kr, ws, wr,
):
    s, d, z, q = place()
    m = s // 2
    core = lax.rem(s, 2)
    wait_barrier = greet(s, z, q, d)
    friend = dp_peer(d, 1)
    gw_all = (gw_v, gw_g)
    loads = [
        pltpu.make_async_copy(a, b, pre.at[i])
        for i, (a, b) in enumerate((
            (counts_in, counts_ref), (w_in, w_ref), (table_in, table),
            (b1_in, b1_ref), (b2_in, b2_ref),
        ))
    ]
    for load in loads:
        load.start()
    scale = 1.0 / math.sqrt(DP * BINS)
    base = s * CH

    def lanes(c):
        return slice(c * TILE, (c + 1) * TILE)

    def krows(c):
        return slice(c * SEQ, (c + 1) * SEQ)

    def put3(c, re, im):
        rh, rl = split(re)
        ih, il = split(im)
        tmp[krows(c), 0:128] = rh
        tmp[krows(c), 128:256] = ih
        tmp[krows(c), 256:384] = rl
        tmp[krows(c), 384:512] = il
        tmp[krows(c), 512:640] = rh
        tmp[krows(c), 640:768] = ih

    def forward(x_ref, dst):
        cr_ = tw_ref[0]
        ci_ = tw_ref[1]
        for p in range(CH // 2):
            x = x_ref[:, p * 256:(p + 1) * 256]
            part = dot(w1_ref[...], jnp.concatenate([x, x], axis=0))
            for h in range(2):
                re = part[0:32, lanes(h)]
                im = part[32:64, lanes(h)]
                put3(2 * p + h, re * cr_ - im * ci_, re * ci_ + im * cr_)
        dst[...] = dot(tmp[...], w2_ref[...])

    def inverse(left, right, conj, emit):
        cr_ = tw_ref[0]
        ci_ = tw_ref[1]
        for c in range(CH):
            lr = left[krows(c), 0:128]
            li = left[krows(c), 128:256]
            rr = right[krows(c), 0:128]
            ri = right[krows(c), 128:256]
            if conj:
                put3(c, lr * rr + li * ri, lr * ri - li * rr)
            else:
                put3(c, lr * rr - li * ri, lr * ri + li * rr)
        inv[...] = dot(tmp[...], v2_ref[...])
        for p in range(CH // 2):
            cols = []
            for h in range(2):
                c = 2 * p + h
                re = inv[krows(c), 0:128]
                im = inv[krows(c), 128:256]
                rh, rl = split(re * cr_ + im * ci_)
                ih, il = split(im * cr_ - re * ci_)
                cols.append(jnp.concatenate([rh, ih, rl, il, rh, ih], axis=0))
            res = dot(v1_ref[...], jnp.concatenate(cols, axis=1))
            for h in range(2):
                emit(2 * p + h, res[:, lanes(h)])

    def z_copy(i):
        return push(own, lev_ref.at[q, z], zs.at[0], zr.at[i], z_peer(z, q, i))

    def x_copy(i):
        slot = lev_ref.at[q, lax.rem(z - i + ZN, ZN)]
        return push(slot, slot, gs.at[0], xr.at[i], q_peer(z, q, 2))

    def g_copy(k, i):
        slot = lev_ref.at[lax.rem(q + k, GROUP), lax.rem(z - i + ZN, ZN)]
        return push(slot, slot, gs.at[0], gr.at[0], core_peer(s))

    def f_copy(i, src, dst, k):
        return push(src, dst.at[d], fs.at[k], fr.at[k], dp_peer(d, 2 * i))

    def fx_copy(src, dst, k):
        return push(src, dst.at[d], fs.at[k], fr.at[2 + k], {"dp": pair(d)})

    def fy_copy(i, dst, k):
        slot = dst.at[pair(d)]
        return push(slot, slot, fs.at[k], fr.at[k], dp_peer(d, 2 * i))

    def far_copy(i, src, mid, k, send, recv):
        to = lax.rem(m + i, SEQ // 2)
        return push(src.at[to], mid.at[m], send.at[k], recv.at[k], same_core(s, i))

    def near_copy(mid, dst, k, send, recv):
        return push(
            mid.at[:, 1 - core], dst.at[:, core], send.at[k], recv.at[k], core_peer(s)
        )

    def h_copy(which, i):
        to = lax.rem(d + i, DP)
        return push(
            gf_s.at[which, to], gf_all.at[which, d], hs.at[which], hr.at[which], dp_peer(d, i)
        )

    def part_rows(part):
        return slice(0, 16) if part == 0 else slice(16, 40)

    def k_copy(part, i):
        at = part_rows(part)
        return push(gwp.at[at], gw_in.at[d, at], ks.at[part], kr.at[part], dp_peer(d, i))

    def wz_copy(part, i):
        slot = gw_all[part].at[m, core]
        return push(slot, slot, ws.at[part], wr.at[part], same_core(s, i))

    def wg_copy(part):
        slot = gw_all[part].at[:, core]
        return push(slot, slot, ws.at[2 + part], wr.at[2 + part], core_peer(s))

    loads[0].wait()
    levels = jnp.log1p(counts_ref[...].astype(f32)) - 3.0
    own[...] = levels.astype(bf16)
    lev_ref[q, z] = own[...]
    wait_barrier()
    for i in LINE:
        z_copy(i).start()

    for i in FAR:
        far_copy(i, cot_in, cot_mid, 0, cs, cr).start()
    fx_copy(f1_in, f1_ref, 0).start()
    fx_copy(f2_in, f2_ref, 1).start()
    x_copy(0).start()
    g_copy(0, 0).start()
    for i in range(1, DP // 2):
        f_copy(i, f1_in, f1_ref, 0).start()
        f_copy(i, f2_in, f2_ref, 1).start()
    keeps = [
        pltpu.make_async_copy(f1_in, f1_ref.at[d], loc.at[0]),
        pltpu.make_async_copy(f2_in, f2_ref.at[d], loc.at[1]),
        pltpu.make_async_copy(cot_in.at[m], cot_mid.at[m], loc.at[2]),
    ]
    for keep in keeps:
        keep.start()
    loads[1].wait()
    wtt[...] = w_ref[...].astype(f32).T
    for k in range(3):
        at = pl.multiple_of(k * D + s * CH, 8)
        wt_ref[k * CH:(k + 1) * CH, :] = wtt[pl.ds(at, CH), :].astype(bf16)
    levs[EVENTS:, :] = jnp.zeros((TILE - EVENTS, BINS), bf16)
    for load in loads[2:]:
        load.wait()
    for at, ref in ((0, w2_ref), (256, v2_ref)):
        hi, lo = split(table[at:at + 256, :])
        ref[0:256, :] = hi
        ref[256:512, :] = hi
        ref[512:768, :] = lo
    hi, lo = split(table[512:576, 0:32])
    w1_ref[...] = jnp.concatenate([hi, lo], axis=1)
    hi, lo = split(table[576:608, 0:64])
    v1_ref[...] = jnp.concatenate([hi, hi, lo], axis=1)
    tw_ref[0] = table[608:640, 0:128]
    tw_ref[1] = table[608:640, 128:256]

    for i in LINE:
        z_copy(i).wait_recv()
        x_copy(i).start()
        g_copy(0, i).start()
    for ref, k in ((f1_ref, 0), (f2_ref, 1)):
        received(ref.at[0], fr.at[2 + k], friend)
        for j in range(1, DP // 2):
            fy_copy(j, ref, k).start()
    for i in (0, *LINE):
        x_copy(i).wait_recv()
        g_copy(2, i).start()

    def load_filter(ref, dst):
        for e in range(DP):
            for p in range(BINS // DP // TILE):
                a = e * (BINS // DP // TILE) + p
                crows[a * CH:(a + 1) * CH, :] = ref[e, :, p * TILE:(p + 1) * TILE].astype(f32)
        for c in range(CH):
            hid[:, lanes(c)] = crows[pl.ds(c, SEQ, stride=CH), :].astype(bf16)
        forward(hid, dst)

    keeps[0].wait()
    received(f1_ref.at[0:DP - 2], fr.at[0], friend)
    load_filter(f1_ref, hat1)
    keeps[1].wait()
    received(f2_ref.at[0:DP - 2], fr.at[1], friend)
    load_filter(f2_ref, hat2)

    received(lev_ref.at[0:2], gr.at[0], friend)
    for a in range(SEQ):
        levs[0:EVENTS, a * TILE:(a + 1) * TILE] = lev_ref[a % GROUP, a // GROUP]
    for p in range(SEQ // 2):
        proj = dot(wt_ref[...], levs[0:EVENTS, p * 256:(p + 1) * 256])
        for h in range(2):
            a = 2 * p + h
            rows[a * COLS:(a + 1) * COLS, :] = proj[:, lanes(h)]
    for c in range(CH):
        val[:, lanes(c)] = rows[pl.ds(c, SEQ, stride=COLS), :].astype(bf16)
        g1[:, lanes(c)] = rows[pl.ds(CH + c, SEQ, stride=COLS), :].astype(bf16)
        g2[:, lanes(c)] = rows[pl.ds(2 * CH + c, SEQ, stride=COLS), :].astype(bf16)
    keeps[2].wait()
    received(cot_mid.at[0:SEQ // 2 - 1], cr.at[0], friend)
    near_copy(cot_mid, cot_ref, 1, cs, cr).start()
    keep_cot = pltpu.make_async_copy(cot_mid.at[:, core], cot_ref.at[:, core], loc.at[3])
    keep_cot.start()
    forward(val, hatv)

    def emit_one(c, conv):
        mixed = rnd(conv) + b1_ref[base + c] * val[:, lanes(c)].astype(f32)
        m1[:, lanes(c)] = mixed
        hid[:, lanes(c)] = (g1[:, lanes(c)].astype(f32) * mixed).astype(bf16)

    inverse(hat1, hatv, False, emit_one)
    forward(hid, hath)

    keep_cot.wait()
    received(cot_ref.at[:, 0], cr.at[1], friend)
    for a in range(SEQ):
        crows[a * CH:(a + 1) * CH, :] = cot_ref[a // 2, a % 2].astype(f32)

    def emit_two(c, conv):
        mixed = rnd(conv) + b2_ref[base + c] * hid[:, lanes(c)].astype(f32)
        up = crows[pl.ds(c, SEQ, stride=CH), :] * scale
        gate = g2[:, lanes(c)].astype(f32)
        rows[pl.ds(2 * CH + c, SEQ, stride=COLS), :] = up * mixed
        m2[:, lanes(c)] = gate * mixed
        gm[:, lanes(c)] = (up * gate).astype(bf16)

    inverse(hat2, hath, False, emit_two)
    for c in range(CH):
        crows[pl.ds(c, SEQ, stride=CH), :] = m2[:, lanes(c)]
    for a in range(SEQ):
        out_s[a // 2, a % 2] = crows[a * CH:(a + 1) * CH, :].astype(bf16)
    for i in FAR:
        far_copy(i, out_s, out_mid, 0, os_, or_).start()
    keep_out = pltpu.make_async_copy(out_s.at[m], out_mid.at[m], loc.at[4])
    keep_out.start()

    def bias_sums(x_ref, y_ref):
        parts = []
        for c in range(CH):
            t = x_ref[:, lanes(c)].astype(f32) * y_ref[:, lanes(c)].astype(f32)
            parts.append(jnp.sum(t, axis=0, keepdims=True))
        return jnp.sum(jnp.concatenate(parts, axis=0), axis=1, keepdims=True)

    def weight_rows(part, sums):
        low, high = ((0, CH), (CH, COLS))[part]
        for a in range(SEQ):
            gpb[low:high, a * TILE:(a + 1) * TILE] = rows[
                a * COLS + low:a * COLS + high, :
            ].astype(bf16)
        weight = lax.dot_general(
            gpb[low:high, :], levs[...], (((1,), (1,)), ((), ())), preferred_element_type=f32
        )
        packed = [
            weight[r:r + 8] + pltpu.roll(weight[r + 8:r + 16], EVENTS, 1)
            for r in range(0, high - low - 8, 16)
        ]
        if part == 0:
            lane = lax.broadcasted_iota(jnp.int32, (8, TILE), 1)
            last = weight[16:24]
            for k, total in enumerate(sums):
                for r in range(3):
                    last = jnp.where(lane == EVENTS + 3 * k + r, total[8 * r:8 * r + 8], last)
            packed.append(last)
        packed = jnp.concatenate(packed, axis=0)
        gwp[part_rows(part), :] = packed
        gw_in[d, part_rows(part), :] = packed

    def total_rows(part):
        total = gw_in[0, part_rows(part), :]
        for k in range(1, DP):
            total = total + gw_in[k, part_rows(part), :]
        gw_all[part][m, core] = total.astype(bf16)

    def emit_gf(which):
        def emit(c, conv):
            gf_s[which, c // 3, :, (c % 3) * TILE:(c % 3 + 1) * TILE] = conv.astype(bf16)
        return emit

    gives = []

    def give(src, dst, k):
        copy = pltpu.make_async_copy(src, dst, done.at[k])
        copy.start()
        gives.append(copy)

    def finish_filter(which, dst):
        received(gf_all.at[which, 0:DP - 1], hr.at[which], friend)
        total = gf_all[which, 0].astype(f32)
        for k in range(1, DP):
            total = total + gf_all[which, k].astype(f32)
        for c in range(3):
            for a in range(SEQ):
                flat[c:c + 1, a * TILE:(a + 1) * TILE] = total[a:a + 1, lanes(c)]
        gf_o[which] = flat[0:3, :].astype(bf16)
        give(gf_o.at[which], dst, which)

    forward(gm, hatg)
    sum_two = bias_sums(gm, hid)

    def emit_carried_two(c, conv):
        ghid = b2_ref[base + c] * gm[:, lanes(c)].astype(f32) + rnd(conv)
        gh[:, lanes(c)] = (ghid * g1[:, lanes(c)].astype(f32)).astype(bf16)
        rows[pl.ds(CH + c, SEQ, stride=COLS), :] = ghid * m1[:, lanes(c)]

    inverse(hat2, hatg, True, emit_carried_two)
    weight_rows(1, ())
    for i in range(1, DP):
        k_copy(1, i).start()

    forward(gh, hat_one_grad)
    sum_one = bias_sums(gh, val)

    def emit_carried_one(c, conv):
        rows[pl.ds(c, SEQ, stride=COLS), :] = (
            b1_ref[base + c] * gh[:, lanes(c)].astype(f32) + rnd(conv)
        )

    inverse(hat1, hat_one_grad, True, emit_carried_one)
    weight_rows(0, (sum_one, sum_two))
    for i in range(1, DP):
        k_copy(0, i).start()

    inverse(hath, hatg, True, emit_gf(1))
    gf_all[1, d] = gf_s[1, d]
    for i in range(1, DP):
        h_copy(1, i).start()

    received(gw_in.at[0:DP - 1, part_rows(1)], kr.at[1], friend)
    total_rows(1)
    for i in FAR:
        wz_copy(1, i).start()
    inverse(hatv, hat_one_grad, True, emit_gf(0))
    gf_all[0, d] = gf_s[0, d]
    for i in range(1, DP):
        h_copy(0, i).start()

    keep_out.wait()
    received(out_mid.at[0:SEQ // 2 - 1], or_.at[0], friend)
    near_copy(out_mid, outg_ref, 1, os_, or_).start()
    keep_plane = pltpu.make_async_copy(out_mid.at[:, core], outg_ref.at[:, core], loc.at[5])
    keep_plane.start()
    received(gw_in.at[0:DP - 1, part_rows(0)], kr.at[0], friend)
    total_rows(0)
    for i in FAR:
        wz_copy(0, i).start()

    def turn(k):
        low = lax.broadcasted_iota(jnp.int32, (8, TILE), 1) < EVENTS
        block = []
        for n in range(SEQ):
            b = gw_all[min(k, 1)][n // 2, n % 2].astype(f32)
            tiles = [b[r:r + 8] for r in range(0, b.shape[0], 8)]
            if k == 0:
                first, last = tiles
                block.append(jnp.where(low, first, last))
                block.append(
                    jnp.where(low, pltpu.roll(first, EVENTS, 1), pltpu.roll(last, TILE - 1, 1))
                )
                block.append(jnp.where(low, last, pltpu.roll(last, TILE - 2, 1)))
            elif k == 1:
                block += [tiles[0], pltpu.roll(tiles[0], EVENTS, 1), tiles[1]]
            else:
                block += [
                    pltpu.roll(tiles[1], EVENTS, 1), tiles[2], pltpu.roll(tiles[2], EVENTS, 1)
                ]
        for p in range(D // TILE):
            turned = jnp.concatenate(block[16 * p:16 * p + 16], axis=0).T
            at = k * D + p * TILE
            gw_o[:, at:at + TILE] = turned[0:EVENTS, :]
            if k == 0:
                gb_o[0:1, p * TILE:(p + 1) * TILE] = turned[EVENTS:EVENTS + 1, :]
                gb_o[1:2, p * TILE:(p + 1) * TILE] = turned[EVENTS + 3:EVENTS + 4, :]
        at = slice(k * D, (k + 1) * D)
        give(gw_o.at[:, at], gwo_ref.at[:, at], 2 + k)

    def pass_weights(part):
        received(gw_all[part].at[0:SEQ // 2 - 1, 0], wr.at[part], friend)
        wg_copy(part).start()

    pass_weights(1)
    finish_filter(1, gf2_ref)
    pass_weights(0)
    finish_filter(0, gf1_ref)
    received(gw_all[1].at[:, 0], wr.at[3], friend)
    turn(1)
    turn(2)
    received(gw_all[0].at[:, 0], wr.at[2], friend)
    turn(0)
    give(gb_o, gb_ref, 5)
    keep_plane.wait()
    received(outg_ref.at[:, 0], or_.at[1], friend)
    sent(lev_ref.at[0, 0:ZN - 1], zs.at[0], friend)
    sent(lev_ref.at[0:GROUP - 1], gs.at[0], friend)
    sent(f1_ref.at[0:DP - 1], fs.at[0], friend)
    sent(f2_ref.at[0:DP - 1], fs.at[1], friend)
    sent(cot_mid.at[0:SEQ // 2 - 1], cs.at[0], friend)
    sent(cot_ref.at[:, 0], cs.at[1], friend)
    sent(out_mid.at[0:SEQ // 2 - 1], os_.at[0], friend)
    sent(outg_ref.at[:, 0], os_.at[1], friend)
    for part in range(2):
        sent(gf_all.at[part, 0:DP - 1], hs.at[part], friend)
        sent(gw_in.at[0:DP - 1, part_rows(part)], ks.at[part], friend)
        sent(gw_all[part].at[0:SEQ // 2 - 1, 0], ws.at[part], friend)
        sent(gw_all[part].at[:, 0], ws.at[2 + part], friend)
    for copy in gives:
        copy.wait()


def whole(counts, w_in, b1, b2, cot, f1, f2):
    dma = pltpu.SemaphoreType.DMA
    vm = pltpu.VMEM
    spec = (SEQ * CH, 2 * TILE)
    return pl.pallas_call(
        whole_kernel,
        out_shape=(
            jax.ShapeDtypeStruct((SEQ // 2, 2, CH, TILE), bf16),
            jax.ShapeDtypeStruct((3, BINS), bf16),
            jax.ShapeDtypeStruct((3, BINS), bf16),
            jax.ShapeDtypeStruct((EVENTS, 3 * D), f32),
            jax.ShapeDtypeStruct((2, D), f32),
        ),
        in_specs=[ANY] * 8,
        out_specs=(ANY,) * 5,
        scratch_shapes=[
            vm((EVENTS, TILE), jnp.int32),
            vm((EVENTS, 3 * D), bf16),
            vm((640, 2 * TILE), f32),
            pltpu.SMEM((D,), f32),
            pltpu.SMEM((D,), f32),
            vm((2 * SEQ, 2 * SEQ), bf16),
            vm((6 * TILE, 2 * TILE), bf16),
            vm((6 * TILE, 2 * TILE), bf16),
            vm((SEQ, 6 * SEQ), bf16),
            vm((2, SEQ, TILE), f32),
            vm((EVENTS, TILE), bf16),
            vm((3 * D, EVENTS), f32),
            vm((COLS, EVENTS), bf16),
            vm((GROUP, ZN, EVENTS, TILE), bf16),
            vm((SEQ // 2, 2, CH, TILE), bf16),
            vm((SEQ // 2, 2, CH, TILE), bf16),
            vm((DP, CH, BINS // DP), bf16),
            vm((DP, CH, BINS // DP), bf16),
            vm((TILE, BINS), bf16),
            vm((SEQ * COLS, TILE), f32),
            vm((SEQ * CH, TILE), f32),
            vm((SEQ, LANES), bf16),
            vm((SEQ, LANES), bf16),
            vm((SEQ, LANES), bf16),
            vm((SEQ, LANES), bf16),
            vm((SEQ, LANES), bf16),
            vm((SEQ, LANES), f32),
            vm((SEQ, LANES), f32),
            vm((SEQ, LANES), bf16),
            vm((SEQ * CH, 6 * TILE), bf16),
            vm(spec, f32),
            vm(spec, f32),
            vm(spec, f32),
            vm(spec, f32),
            vm(spec, f32),
            vm(spec, f32),
            vm(spec, f32),
            vm((COLS, BINS), bf16),
            vm((SEQ // 2, 2, CH, TILE), bf16),
            vm((SEQ // 2, 2, CH, TILE), bf16),
            vm((2, DP, SEQ, 3 * TILE), bf16),
            vm((40, TILE), f32),
            vm((2, DP, SEQ, 3 * TILE), bf16),
            vm((DP, 40, TILE), f32),
            vm((SEQ // 2, 2, 16, TILE), bf16),
            vm((SEQ // 2, 2, 24, TILE), bf16),
            vm((8, BINS), f32),
            vm((2, 3, BINS), bf16),
            vm((EVENTS, 3 * D), f32),
            vm((2, D), f32),
            dma((5,)),
            dma((6,)),
            dma((6,)),
            dma((8,)),
            dma((8,)),
            dma((1,)),
            dma((1,)),
            dma((1,)),
            dma((2,)),
            dma((4,)),
            dma((2,)),
            dma((2,)),
            dma((2,)),
            dma((2,)),
            dma((2,)),
            dma((2,)),
            dma((2,)),
            dma((2,)),
            dma((4,)),
            dma((4,)),
        ],
        compiler_params=pltpu.CompilerParams(
            collective_id=0, has_side_effects=True, vmem_limit_bytes=LIMIT
        ),
        name="whole",
    )(counts, w_in, b1, b2, cot, f1, f2, tables())


def finish_kernel(
    out_in, gf1_in, gf2_in, gw_in, gb_in, out_ref, gf1_ref, gf2_ref, gw_ref, gb1_ref, gb2_ref
):
    out_ref[...] = out_in[...]
    gf1_ref[...] = gf1_in[...]
    gf2_ref[...] = gf2_in[...]
    gw_ref[...] = gw_in[...]
    gb1_ref[...] = gb_in[0]
    gb2_ref[...] = gb_in[1]


def finish(out, gf1, gf2, gw, gb):
    like = [jax.ShapeDtypeStruct(x.shape, x.dtype) for x in (out, gf1, gf2, gw)]
    flat = jax.ShapeDtypeStruct((D,), f32)
    return pl.pallas_call(
        finish_kernel,
        out_shape=(*like, flat, flat),
        in_specs=[VMEM] * 5,
        out_specs=(VMEM,) * 6,
        compiler_params=pltpu.CompilerParams(vmem_limit_bytes=LIMIT),
        name="finish",
    )(out, gf1, gf2, gw, gb)


def body(counts, w_in, bias_one, bias_two, filter_one, filter_two, cotangent):
    out, gf1, gf2, gw, gb = whole(
        counts[0].T, w_in, bias_one, bias_two, cotangent.reshape(SEQ // 2, 2, CH, TILE),
        filter_one, filter_two,
    )
    out, gf1, gf2, gw, gb1, gb2 = finish(out.reshape(1, D, TILE), gf1, gf2, gw, gb)
    return out, gw, gb1, gb2, gf1, gf2


def solution(mesh):
    return jax.shard_map(
        body,
        mesh=mesh,
        in_specs=(
            P("dp", "seq", None),
            P(),
            P(),
            P(),
            P("seq", "dp"),
            P("seq", "dp"),
            P("dp", None, "seq"),
        ),
        out_specs=(
            P("dp", None, "seq"),
            P(),
            P(),
            P(),
            P(("seq", "dp"), None),
            P(("seq", "dp"), None),
        ),
        check_vma=False,
    )
```

```python
import functools
import math

import jax
import jax.numpy as jnp
import numpy as np
from jax import lax
from jax.experimental import pallas as pl
from jax.experimental.pallas import tpu as pltpu
from jax.sharding import PartitionSpec as P

SEQ = 32
DP = 8
ZN = 8
GROUP = 4
TILE = 128
EVENTS = 64
CH = 24
D = SEQ * CH
BINS = SEQ * TILE
COLS = 3 * CH
LANES = CH * TILE
f32 = jnp.float32
bf16 = jnp.bfloat16
MESH = pl.DeviceIdType.MESH
VMEM = pl.BlockSpec(memory_space=pltpu.VMEM)
SMEM = pl.BlockSpec(memory_space=pltpu.SMEM)
ANY = pl.BlockSpec(memory_space=pl.ANY)
LIMIT = 56 * 1024 * 1024
LINE = (4, 3, 5, 2, 6, 1, 7)
FAR = (8, 7, 9, 6, 10, 5, 11, 4, 12, 3, 13, 2, 14, 1, 15)


def tables():
    a = np.arange(SEQ)
    j = np.arange(TILE)
    k1 = np.arange(SEQ) + 0.25
    k2 = np.arange(TILE)
    first = np.exp(-2j * np.pi * np.outer(k1, a) / SEQ)
    turn = np.exp(-2j * np.pi * np.outer(k1, j) / BINS)
    second = np.exp(-2j * np.pi * np.outer(j, k2) / TILE)
    w1 = np.concatenate([first.real, first.imag], axis=0)
    w2 = np.block([[second.real, second.imag], [-second.imag, second.real]])
    inv2 = np.conj(second).T
    v2 = np.block([[inv2.real, inv2.imag], [-inv2.imag, inv2.real]])
    last = np.conj(first).T / BINS
    v1 = np.concatenate([last.real, -last.imag], axis=1)

    table = np.zeros((640, 2 * TILE), np.float32)
    table[0:256] = w2
    table[256:512] = v2
    table[512:576, 0:32] = w1
    table[576:608, 0:64] = v1
    table[608:640, 0:128] = turn.real
    table[608:640, 128:256] = turn.imag
    return table


def dot(x, y):
    return jnp.dot(x, y, preferred_element_type=f32)


def split(x):
    hi = x.astype(bf16)
    lo = (x - hi.astype(f32)).astype(bf16)
    return hi, lo


def rnd(x):
    return x.astype(bf16).astype(f32)


def place():
    s = lax.axis_index("seq")
    d = lax.axis_index("dp")
    return s, d, s // GROUP, lax.rem(s, GROUP)


def dp_peer(d, i):
    return {"dp": lax.rem(d + i, DP)}


def z_peer(z, q, i):
    return {"seq": lax.rem(z + i, ZN) * GROUP + q}


def q_peer(z, q, r):
    return {"seq": z * GROUP + lax.rem(q + r, GROUP)}


def push(src, dst, send, recv, device):
    return pltpu.make_async_remote_copy(
        src_ref=src, dst_ref=dst, send_sem=send, recv_sem=recv,
        device_id=device, device_id_type=MESH,
    )


def same_core(s, i):
    return {"seq": lax.rem(s + 2 * i, SEQ)}


def core_peer(s):
    return {"seq": s + 1 - 2 * lax.rem(s, 2)}


def pair(d):
    return d + 1 - 2 * lax.rem(d, 2)


def greet(s, z, q, d):
    barrier = pltpu.get_barrier_semaphore()

    def hello(device):
        pl.semaphore_signal(barrier, inc=1, device_id=device, device_id_type=MESH)

    for i in FAR:
        hello(same_core(s, i))
    hello(core_peer(s))
    for i in range(1, DP):
        hello(dp_peer(d, i))
    return lambda: pl.semaphore_wait(barrier, SEQ // 2 + DP - 1)


def received(ref, sem, device):
    push(ref, ref, sem, sem, device).wait_recv()


def sent(ref, sem, device):
    push(ref, ref, sem, sem, device).wait_send()


def each(low, high, f):
    def step(i, _):
        f(i)
        return 0

    lax.fori_loop(low, high, step, 0)


def whole_kernel(
    counts_in, w_in, b1_in, b2_in, cot_in, f1_in, f2_in, table_in,
    outg_ref, gf1_ref, gf2_ref, gwo_ref, gwv_ref,
    counts_ref, w_ref, table, b1_ref, b2_ref, w1_ref, w2_ref, v2_ref, v1_ref, tw_ref,
    own, wtt, wt_ref, lev_ref, cot_mid, cot_ref, f1_ref, f2_ref,
    levs, rows, crows, val, g1, g2, hid, gm, m1, m2, gh,
    tmp, inv, hat1, hat2, hatv, hath, hatg, hat_one_grad, gpb,
    out_s, out_mid, gf_s, gwp, gf_all, gw_in, gw_v, gw_g, flat, gf_o, gw_o,
    pre, loc, done, zr, xr, zs, gs, gr, fs, fr, cs, cr, os_, or_, hs, hr, ks, kr, ws, wr,
):
    s, d, z, q = place()
    m = s // 2
    core = lax.rem(s, 2)
    wait_barrier = greet(s, z, q, d)
    friend = dp_peer(d, 1)
    gw_all = (gw_v, gw_g)
    loads = [
        pltpu.make_async_copy(a, b, pre.at[i])
        for i, (a, b) in enumerate((
            (counts_in, counts_ref), (w_in, w_ref), (table_in, table),
            (b1_in, b1_ref), (b2_in, b2_ref),
        ))
    ]
    for load in loads:
        load.start()
    scale = 1.0 / math.sqrt(DP * BINS)
    base = s * CH

    def lanes(c):
        return slice(c * TILE, (c + 1) * TILE)

    def krows(c):
        return slice(c * SEQ, (c + 1) * SEQ)

    def put3(c, re, im):
        tmp[krows(c), 0:128] = re.astype(bf16)
        tmp[krows(c), 128:256] = im.astype(bf16)

    def forward(x_ref, dst):
        cr_ = tw_ref[0]
        ci_ = tw_ref[1]
        for p in range(CH // 2):
            x = x_ref[:, p * 256:(p + 1) * 256]
            part = dot(w1_ref[...], jnp.concatenate([x, x], axis=0))
            for h in range(2):
                re = part[0:32, lanes(h)]
                im = part[32:64, lanes(h)]
                put3(2 * p + h, re * cr_ - im * ci_, re * ci_ + im * cr_)
        dst[...] = dot(tmp[...], w2_ref[0:256, :]) + dot(tmp[...], w2_ref[256:512, :])

    def inverse(left, right, conj, emit):
        cr_ = tw_ref[0]
        ci_ = tw_ref[1]
        for c in range(CH):
            lr = left[krows(c), 0:128]
            li = left[krows(c), 128:256]
            rr = right[krows(c), 0:128]
            ri = right[krows(c), 128:256]
            if conj:
                put3(c, lr * rr + li * ri, lr * ri - li * rr)
            else:
                put3(c, lr * rr - li * ri, lr * ri + li * rr)
        inv[...] = dot(tmp[...], v2_ref[0:256, :]) + dot(tmp[...], v2_ref[256:512, :])
        for p in range(CH // 2):
            cols = []
            for h in range(2):
                c = 2 * p + h
                re = inv[krows(c), 0:128]
                im = inv[krows(c), 128:256]
                rh = (re * cr_ + im * ci_).astype(bf16)
                ih = (im * cr_ - re * ci_).astype(bf16)
                cols.append(jnp.concatenate([rh, ih, rh, ih], axis=0))
            res = dot(v1_ref[...], jnp.concatenate(cols, axis=1))
            for h in range(2):
                emit(2 * p + h, res[:, lanes(h)])

    def z_copy(i):
        return push(own, lev_ref.at[q, z], zs.at[0], zr.at[i], z_peer(z, q, i))

    def x_copy(i):
        slot = lev_ref.at[q, lax.rem(z - i + ZN, ZN)]
        return push(slot, slot, gs.at[0], xr.at[i], q_peer(z, q, 2))

    def g_copy(k, i):
        slot = lev_ref.at[lax.rem(q + k, GROUP), lax.rem(z - i + ZN, ZN)]
        return push(slot, slot, gs.at[0], gr.at[0], core_peer(s))

    def f_copy(i, src, dst, k):
        return push(src, dst.at[d], fs.at[k], fr.at[k], dp_peer(d, 2 * i))

    def fx_copy(src, dst, k):
        return push(src, dst.at[d], fs.at[k], fr.at[2 + k], {"dp": pair(d)})

    def fy_copy(i, dst, k):
        slot = dst.at[pair(d)]
        return push(slot, slot, fs.at[k], fr.at[k], dp_peer(d, 2 * i))

    def far_copy(i, src, mid, k, send, recv):
        to = lax.rem(m + i, SEQ // 2)
        return push(src.at[to], mid.at[m], send.at[k], recv.at[k], same_core(s, i))

    def near_copy(mid, dst, k, send, recv):
        return push(
            mid.at[:, 1 - core], dst.at[:, core], send.at[k], recv.at[k], core_peer(s)
        )

    def h_copy(which, i):
        to = lax.rem(d + i, DP)
        return push(
            gf_s.at[which, to], gf_all.at[which, d], hs.at[which], hr.at[which], dp_peer(d, i)
        )

    def part_rows(part):
        return slice(0, 16) if part == 0 else slice(16, 40)

    def k_copy(part, i):
        at = part_rows(part)
        return push(gwp.at[at], gw_in.at[d, at], ks.at[part], kr.at[part], dp_peer(d, i))

    def wz_copy(part, i):
        slot = gw_all[part].at[m, core]
        return push(slot, slot, ws.at[part], wr.at[part], same_core(s, i))

    def wg_copy(part):
        slot = gw_all[part].at[:, core]
        dst = gwv_ref.at[:, core] if part == 0 else slot
        return push(slot, dst, ws.at[2 + part], wr.at[2 + part], core_peer(s))

    loads[0].wait()
    levels = jnp.log1p(counts_ref[...].astype(f32)) - 3.0
    own[...] = levels.astype(bf16)
    lev_ref[q, z] = own[...]
    wait_barrier()
    for i in LINE:
        z_copy(i).start()

    x_copy(0).start()
    g_copy(0, 0).start()
    fx_copy(f1_in, f1_ref, 0).start()
    fx_copy(f2_in, f2_ref, 1).start()
    for i in FAR:
        far_copy(i, cot_in, cot_mid, 0, cs, cr).start()
    for i in range(1, DP // 2):
        f_copy(i, f1_in, f1_ref, 0).start()
        f_copy(i, f2_in, f2_ref, 1).start()
    keeps = [
        pltpu.make_async_copy(f1_in, f1_ref.at[d], loc.at[0]),
        pltpu.make_async_copy(f2_in, f2_ref.at[d], loc.at[1]),
        pltpu.make_async_copy(cot_in.at[m], cot_mid.at[m], loc.at[2]),
    ]
    for keep in keeps:
        keep.start()
    loads[1].wait()
    wtt[...] = w_ref[...].astype(f32).T
    for k in range(3):
        at = pl.multiple_of(k * D + s * CH, 8)
        wt_ref[k * CH:(k + 1) * CH, :] = wtt[pl.ds(at, CH), :].astype(bf16)
    levs[EVENTS:, :] = jnp.zeros((TILE - EVENTS, BINS), bf16)
    for load in loads[2:]:
        load.wait()
    for at, ref in ((0, w2_ref), (256, v2_ref)):
        hi, lo = split(table[at:at + 256, :])
        ref[0:256, :] = hi
        ref[256:512, :] = lo
    hi, lo = split(table[512:576, 0:32])
    w1_ref[...] = jnp.concatenate([hi, lo], axis=1)
    hi, lo = split(table[576:608, 0:64])
    v1_ref[...] = jnp.concatenate([hi, lo], axis=1)
    tw_ref[0] = table[608:640, 0:128]
    tw_ref[1] = table[608:640, 128:256]

    for i in LINE:
        z_copy(i).wait_recv()
        x_copy(i).start()
        g_copy(0, i).start()
    for ref, k in ((f1_ref, 0), (f2_ref, 1)):
        received(ref.at[0], fr.at[2 + k], friend)
        for j in range(1, DP // 2):
            fy_copy(j, ref, k).start()
    for i in (0, *LINE):
        x_copy(i).wait_recv()
        g_copy(2, i).start()

    def load_filter(ref, dst):
        for e in range(DP):
            for p in range(BINS // DP // TILE):
                a = e * (BINS // DP // TILE) + p
                crows[a * CH:(a + 1) * CH, :] = ref[e, :, p * TILE:(p + 1) * TILE].astype(f32)
        for c in range(CH):
            hid[:, lanes(c)] = crows[pl.ds(c, SEQ, stride=CH), :].astype(bf16)
        forward(hid, dst)

    keeps[0].wait()
    received(f1_ref.at[0:DP - 2], fr.at[0], friend)
    load_filter(f1_ref, hat1)
    keeps[1].wait()
    received(f2_ref.at[0:DP - 2], fr.at[1], friend)
    load_filter(f2_ref, hat2)

    received(lev_ref.at[0:2], gr.at[0], friend)
    for a in range(SEQ):
        levs[0:EVENTS, a * TILE:(a + 1) * TILE] = lev_ref[a % GROUP, a // GROUP]
    for p in range(SEQ // 2):
        proj = dot(wt_ref[...], levs[0:EVENTS, p * 256:(p + 1) * 256])
        for h in range(2):
            a = 2 * p + h
            rows[a * COLS:(a + 1) * COLS, :] = proj[:, lanes(h)]
    for c in range(CH):
        val[:, lanes(c)] = rows[pl.ds(c, SEQ, stride=COLS), :].astype(bf16)
        g1[:, lanes(c)] = rows[pl.ds(CH + c, SEQ, stride=COLS), :].astype(bf16)
        g2[:, lanes(c)] = rows[pl.ds(2 * CH + c, SEQ, stride=COLS), :].astype(bf16)
    keeps[2].wait()
    received(cot_mid.at[0:SEQ // 2 - 1], cr.at[0], friend)
    near_copy(cot_mid, cot_ref, 1, cs, cr).start()
    keep_cot = pltpu.make_async_copy(cot_mid.at[:, core], cot_ref.at[:, core], loc.at[3])
    keep_cot.start()
    forward(val, hatv)

    def emit_one(c, conv):
        mixed = rnd(conv) + b1_ref[base + c] * val[:, lanes(c)].astype(f32)
        m1[:, lanes(c)] = mixed
        hid[:, lanes(c)] = (g1[:, lanes(c)].astype(f32) * mixed).astype(bf16)

    inverse(hat1, hatv, False, emit_one)
    forward(hid, hath)

    keep_cot.wait()
    received(cot_ref.at[:, 0], cr.at[1], friend)
    for a in range(SEQ):
        crows[a * CH:(a + 1) * CH, :] = cot_ref[a // 2, a % 2].astype(f32)

    def emit_two(c, conv):
        mixed = rnd(conv) + b2_ref[base + c] * hid[:, lanes(c)].astype(f32)
        up = crows[pl.ds(c, SEQ, stride=CH), :] * scale
        gate = g2[:, lanes(c)].astype(f32)
        rows[pl.ds(2 * CH + c, SEQ, stride=COLS), :] = up * mixed
        m2[:, lanes(c)] = gate * mixed
        gm[:, lanes(c)] = (up * gate).astype(bf16)

    inverse(hat2, hath, False, emit_two)
    for c in range(CH):
        crows[pl.ds(c, SEQ, stride=CH), :] = m2[:, lanes(c)]
    for a in range(SEQ):
        out_s[a // 2, a % 2] = crows[a * CH:(a + 1) * CH, :].astype(bf16)
    for i in FAR:
        far_copy(i, out_s, out_mid, 0, os_, or_).start()
    keep_out = pltpu.make_async_copy(out_s.at[m], out_mid.at[m], loc.at[4])
    keep_out.start()

    def bias_sums(x_ref, y_ref):
        parts = []
        for c in range(CH):
            t = x_ref[:, lanes(c)].astype(f32) * y_ref[:, lanes(c)].astype(f32)
            parts.append(jnp.sum(t, axis=0, keepdims=True))
        return jnp.sum(jnp.concatenate(parts, axis=0), axis=1, keepdims=True)

    def weight_rows(part, sums):
        low, high = ((0, CH), (CH, COLS))[part]
        for a in range(SEQ):
            gpb[low:high, a * TILE:(a + 1) * TILE] = rows[
                a * COLS + low:a * COLS + high, :
            ].astype(bf16)
        weight = lax.dot_general(
            gpb[low:high, :], levs[...], (((1,), (1,)), ((), ())), preferred_element_type=f32
        )
        packed = [
            weight[r:r + 8] + pltpu.roll(weight[r + 8:r + 16], EVENTS, 1)
            for r in range(0, high - low - 8, 16)
        ]
        if part == 0:
            lane = lax.broadcasted_iota(jnp.int32, (8, TILE), 1)
            last = weight[16:24]
            for k, total in enumerate(sums):
                for r in range(3):
                    last = jnp.where(lane == EVENTS + 3 * k + r, total[8 * r:8 * r + 8], last)
            packed.append(last)
        packed = jnp.concatenate(packed, axis=0)
        gwp[part_rows(part), :] = packed
        gw_in[d, part_rows(part), :] = packed

    def total_rows(part):
        total = gw_in[0, part_rows(part), :]
        for k in range(1, DP):
            total = total + gw_in[k, part_rows(part), :]
        gw_all[part][m, core] = total.astype(bf16)

    def emit_gf(which):
        def emit(c, conv):
            gf_s[which, c // 3, :, (c % 3) * TILE:(c % 3 + 1) * TILE] = conv.astype(bf16)
        return emit

    gives = []

    def give(src, dst, k):
        copy = pltpu.make_async_copy(src, dst, done.at[k])
        copy.start()
        gives.append(copy)

    def finish_filter(which, dst):
        received(gf_all.at[which, 0:DP - 1], hr.at[which], friend)
        total = gf_all[which, 0].astype(f32)
        for k in range(1, DP):
            total = total + gf_all[which, k].astype(f32)
        for c in range(3):
            for a in range(SEQ):
                flat[c:c + 1, a * TILE:(a + 1) * TILE] = total[a:a + 1, lanes(c)]
        gf_o[which] = flat[0:3, :].astype(bf16)
        give(gf_o.at[which], dst, which)

    forward(gm, hatg)
    sum_two = bias_sums(gm, hid)

    def emit_carried_two(c, conv):
        ghid = b2_ref[base + c] * gm[:, lanes(c)].astype(f32) + rnd(conv)
        gh[:, lanes(c)] = (ghid * g1[:, lanes(c)].astype(f32)).astype(bf16)
        rows[pl.ds(CH + c, SEQ, stride=COLS), :] = ghid * m1[:, lanes(c)]

    inverse(hat2, hatg, True, emit_carried_two)
    weight_rows(1, ())
    for i in range(1, DP):
        k_copy(1, i).start()

    forward(gh, hat_one_grad)
    sum_one = bias_sums(gh, val)

    def emit_carried_one(c, conv):
        rows[pl.ds(c, SEQ, stride=COLS), :] = (
            b1_ref[base + c] * gh[:, lanes(c)].astype(f32) + rnd(conv)
        )

    inverse(hat1, hat_one_grad, True, emit_carried_one)
    weight_rows(0, (sum_one, sum_two))
    for i in range(1, DP):
        k_copy(0, i).start()

    inverse(hath, hatg, True, emit_gf(1))
    gf_all[1, d] = gf_s[1, d]
    for i in range(1, DP):
        h_copy(1, i).start()

    received(gw_in.at[0:DP - 1, part_rows(1)], kr.at[1], friend)
    total_rows(1)
    for i in FAR:
        wz_copy(1, i).start()
    inverse(hatv, hat_one_grad, True, emit_gf(0))
    gf_all[0, d] = gf_s[0, d]
    for i in range(1, DP):
        h_copy(0, i).start()

    keep_out.wait()
    received(out_mid.at[0:SEQ // 2 - 1], or_.at[0], friend)
    near_copy(out_mid, outg_ref, 1, os_, or_).start()
    keep_plane = pltpu.make_async_copy(out_mid.at[:, core], outg_ref.at[:, core], loc.at[5])
    keep_plane.start()
    received(gw_in.at[0:DP - 1, part_rows(0)], kr.at[0], friend)
    total_rows(0)
    for i in FAR:
        wz_copy(0, i).start()

    def turn(k):
        block = []
        for n in range(SEQ):
            b = gw_g[n // 2, n % 2].astype(f32)
            tiles = [b[r:r + 8] for r in range(0, 24, 8)]
            if k == 1:
                block += [tiles[0], pltpu.roll(tiles[0], EVENTS, 1), tiles[1]]
            else:
                block += [
                    pltpu.roll(tiles[1], EVENTS, 1), tiles[2], pltpu.roll(tiles[2], EVENTS, 1)
                ]
        for p in range(D // TILE):
            turned = jnp.concatenate(block[16 * p:16 * p + 16], axis=0).T
            at = (k - 1) * D + p * TILE
            gw_o[:, at:at + TILE] = turned[0:EVENTS, :]

    def pass_weights(part):
        received(gw_all[part].at[0:SEQ // 2 - 1, 0], wr.at[part], friend)
        wg_copy(part).start()

    pass_weights(1)
    finish_filter(1, gf2_ref)
    received(gw_all[1].at[:, 0], wr.at[3], friend)
    turn(1)
    turn(2)
    give(gw_o, gwo_ref, 2)
    pass_weights(0)
    give(gw_v.at[:, core], gwv_ref.at[:, core], 3)
    finish_filter(0, gf1_ref)
    received(gw_v.at[:, 0], wr.at[2], friend)
    keep_plane.wait()
    received(outg_ref.at[:, 0], or_.at[1], friend)
    sent(lev_ref.at[0, 0:ZN - 1], zs.at[0], friend)
    sent(lev_ref.at[0:GROUP - 1], gs.at[0], friend)
    sent(f1_ref.at[0:DP - 1], fs.at[0], friend)
    sent(f2_ref.at[0:DP - 1], fs.at[1], friend)
    sent(cot_mid.at[0:SEQ // 2 - 1], cs.at[0], friend)
    sent(cot_ref.at[:, 0], cs.at[1], friend)
    sent(out_mid.at[0:SEQ // 2 - 1], os_.at[0], friend)
    sent(outg_ref.at[:, 0], os_.at[1], friend)
    for part in range(2):
        sent(gf_all.at[part, 0:DP - 1], hs.at[part], friend)
        sent(gw_in.at[0:DP - 1, part_rows(part)], ks.at[part], friend)
        sent(gw_all[part].at[0:SEQ // 2 - 1, 0], ws.at[part], friend)
        sent(gw_all[part].at[:, 0], ws.at[2 + part], friend)
    for copy in gives:
        copy.wait()


def whole(counts, w_in, b1, b2, cot, f1, f2):
    dma = pltpu.SemaphoreType.DMA
    vm = pltpu.VMEM
    spec = (SEQ * CH, 2 * TILE)
    return pl.pallas_call(
        whole_kernel,
        out_shape=(
            jax.ShapeDtypeStruct((SEQ // 2, 2, CH, TILE), bf16),
            jax.ShapeDtypeStruct((3, BINS), bf16),
            jax.ShapeDtypeStruct((3, BINS), bf16),
            jax.ShapeDtypeStruct((EVENTS, 2 * D), f32),
            jax.ShapeDtypeStruct((SEQ // 2, 2, 16, TILE), bf16),
        ),
        in_specs=[ANY] * 8,
        out_specs=(ANY,) * 5,
        scratch_shapes=[
            vm((EVENTS, TILE), jnp.int32),
            vm((EVENTS, 3 * D), bf16),
            vm((640, 2 * TILE), f32),
            pltpu.SMEM((D,), f32),
            pltpu.SMEM((D,), f32),
            vm((2 * SEQ, 2 * SEQ), bf16),
            vm((4 * TILE, 2 * TILE), bf16),
            vm((4 * TILE, 2 * TILE), bf16),
            vm((SEQ, 4 * SEQ), bf16),
            vm((2, SEQ, TILE), f32),
            vm((EVENTS, TILE), bf16),
            vm((3 * D, EVENTS), f32),
            vm((COLS, EVENTS), bf16),
            vm((GROUP, ZN, EVENTS, TILE), bf16),
            vm((SEQ // 2, 2, CH, TILE), bf16),
            vm((SEQ // 2, 2, CH, TILE), bf16),
            vm((DP, CH, BINS // DP), bf16),
            vm((DP, CH, BINS // DP), bf16),
            vm((TILE, BINS), bf16),
            vm((SEQ * COLS, TILE), f32),
            vm((SEQ * CH, TILE), f32),
            vm((SEQ, LANES), bf16),
            vm((SEQ, LANES), bf16),
            vm((SEQ, LANES), bf16),
            vm((SEQ, LANES), bf16),
            vm((SEQ, LANES), bf16),
            vm((SEQ, LANES), f32),
            vm((SEQ, LANES), f32),
            vm((SEQ, LANES), bf16),
            vm((SEQ * CH, 2 * TILE), bf16),
            vm(spec, f32),
            vm(spec, f32),
            vm(spec, f32),
            vm(spec, f32),
            vm(spec, f32),
            vm(spec, f32),
            vm(spec, f32),
            vm((COLS, BINS), bf16),
            vm((SEQ // 2, 2, CH, TILE), bf16),
            vm((SEQ // 2, 2, CH, TILE), bf16),
            vm((2, DP, SEQ, 3 * TILE), bf16),
            vm((40, TILE), f32),
            vm((2, DP, SEQ, 3 * TILE), bf16),
            vm((DP, 40, TILE), f32),
            vm((SEQ // 2, 2, 16, TILE), bf16),
            vm((SEQ // 2, 2, 24, TILE), bf16),
            vm((8, BINS), f32),
            vm((2, 3, BINS), bf16),
            vm((EVENTS, 2 * D), f32),
            dma((5,)),
            dma((6,)),
            dma((6,)),
            dma((8,)),
            dma((8,)),
            dma((1,)),
            dma((1,)),
            dma((1,)),
            dma((2,)),
            dma((4,)),
            dma((2,)),
            dma((2,)),
            dma((2,)),
            dma((2,)),
            dma((2,)),
            dma((2,)),
            dma((2,)),
            dma((2,)),
            dma((4,)),
            dma((4,)),
        ],
        compiler_params=pltpu.CompilerParams(
            collective_id=0, has_side_effects=True, vmem_limit_bytes=LIMIT
        ),
        name="whole",
    )(counts, w_in, b1, b2, cot, f1, f2, tables())


def finish_kernel(
    out_in, gf1_in, gf2_in, gates_in, value_in,
    out_ref, gf1_ref, gf2_ref, gw_ref, gb1_ref, gb2_ref,
):
    low = lax.broadcasted_iota(jnp.int32, (8, TILE), 1) < EVENTS
    block = []
    for n in range(SEQ):
        b = value_in[n // 2, n % 2].astype(f32)
        first, last = b[0:8], b[8:16]
        block.append(jnp.where(low, first, last))
        block.append(
            jnp.where(low, pltpu.roll(first, EVENTS, 1), pltpu.roll(last, TILE - 1, 1))
        )
        block.append(jnp.where(low, last, pltpu.roll(last, TILE - 2, 1)))
    for p in range(D // TILE):
        turned = jnp.concatenate(block[16 * p:16 * p + 16], axis=0).T
        at = slice(p * TILE, (p + 1) * TILE)
        gw_ref[:, at] = turned[0:EVENTS, :]
        gb1_ref[at] = turned[EVENTS]
        gb2_ref[at] = turned[EVENTS + 3]
    gw_ref[:, D:] = gates_in[...]
    out_ref[...] = out_in[...]
    gf1_ref[...] = gf1_in[...]
    gf2_ref[...] = gf2_in[...]


def finish(out, gf1, gf2, gates, value):
    def like(x):
        return jax.ShapeDtypeStruct(x.shape, x.dtype)

    flat = jax.ShapeDtypeStruct((D,), f32)
    return pl.pallas_call(
        finish_kernel,
        out_shape=(
            like(out), like(gf1), like(gf2), jax.ShapeDtypeStruct((EVENTS, 3 * D), f32), flat, flat
        ),
        in_specs=[VMEM] * 5,
        out_specs=(VMEM,) * 6,
        compiler_params=pltpu.CompilerParams(vmem_limit_bytes=LIMIT),
        name="finish",
    )(out, gf1, gf2, gates, value)


def body(counts, w_in, bias_one, bias_two, filter_one, filter_two, cotangent):
    out, gf1, gf2, gates, value = whole(
        counts[0].T, w_in, bias_one, bias_two, cotangent.reshape(SEQ // 2, 2, CH, TILE),
        filter_one, filter_two,
    )
    out, gf1, gf2, gw, gb1, gb2 = finish(out.reshape(1, D, TILE), gf1, gf2, gates, value)
    return out, gw, gb1, gb2, gf1, gf2


def solution(mesh):
    return jax.shard_map(
        body,
        mesh=mesh,
        in_specs=(
            P("dp", "seq", None),
            P(),
            P(),
            P(),
            P("seq", "dp"),
            P("seq", "dp"),
            P("dp", None, "seq"),
        ),
        out_specs=(
            P("dp", None, "seq"),
            P(),
            P(),
            P(),
            P(("seq", "dp"), None),
            P(("seq", "dp"), None),
        ),
        check_vma=False,
    )
```

```python
import functools
import math

import jax
import jax.numpy as jnp
import numpy as np
from jax import lax
from jax.experimental import pallas as pl
from jax.experimental.pallas import tpu as pltpu
from jax.sharding import PartitionSpec as P

SEQ = 32
DP = 8
ZN = 8
GROUP = 4
TILE = 128
EVENTS = 64
CH = 24
D = SEQ * CH
BINS = SEQ * TILE
COLS = 3 * CH
LANES = CH * TILE
f32 = jnp.float32
bf16 = jnp.bfloat16
MESH = pl.DeviceIdType.MESH
VMEM = pl.BlockSpec(memory_space=pltpu.VMEM)
SMEM = pl.BlockSpec(memory_space=pltpu.SMEM)
ANY = pl.BlockSpec(memory_space=pl.ANY)
LIMIT = 56 * 1024 * 1024
LINE = (4, 3, 5, 2, 6, 1, 7)
FAR = (8, 7, 9, 6, 10, 5, 11, 4, 12, 3, 13, 2, 14, 1, 15)


def tables():
    a = np.arange(SEQ)
    j = np.arange(TILE)
    k1 = np.arange(SEQ) + 0.25
    k2 = np.arange(TILE)
    first = np.exp(-2j * np.pi * np.outer(k1, a) / SEQ)
    turn = np.exp(-2j * np.pi * np.outer(k1, j) / BINS)
    second = np.exp(-2j * np.pi * np.outer(j, k2) / TILE)
    w1 = np.concatenate([first.real, first.imag], axis=0)
    w2 = np.block([[second.real, second.imag], [-second.imag, second.real]])
    inv2 = np.conj(second).T
    v2 = np.block([[inv2.real, inv2.imag], [-inv2.imag, inv2.real]])
    last = np.conj(first).T / BINS
    v1 = np.concatenate([last.real, -last.imag], axis=1)

    table = np.zeros((640, 2 * TILE), np.float32)
    table[0:256] = w2
    table[256:512] = v2
    table[512:576, 0:32] = w1
    table[576:608, 0:64] = v1
    table[608:640, 0:128] = turn.real
    table[608:640, 128:256] = turn.imag
    return table


def dot(x, y):
    return jnp.dot(x, y, preferred_element_type=f32)


def split(x):
    hi = x.astype(bf16)
    lo = (x - hi.astype(f32)).astype(bf16)
    return hi, lo


def rnd(x):
    return x.astype(bf16).astype(f32)


def place():
    s = lax.axis_index("seq")
    d = lax.axis_index("dp")
    return s, d, s // GROUP, lax.rem(s, GROUP)


def dp_peer(d, i):
    return {"dp": lax.rem(d + i, DP)}


def z_peer(z, q, i):
    return {"seq": lax.rem(z + i, ZN) * GROUP + q}


def q_peer(z, q, r):
    return {"seq": z * GROUP + lax.rem(q + r, GROUP)}


def push(src, dst, send, recv, device):
    return pltpu.make_async_remote_copy(
        src_ref=src, dst_ref=dst, send_sem=send, recv_sem=recv,
        device_id=device, device_id_type=MESH,
    )


def same_core(s, i):
    return {"seq": lax.rem(s + 2 * i, SEQ)}


def core_peer(s):
    return {"seq": s + 1 - 2 * lax.rem(s, 2)}


def pair(d):
    return d + 1 - 2 * lax.rem(d, 2)


def greet(s, z, q, d):
    barrier = pltpu.get_barrier_semaphore()

    def hello(device):
        pl.semaphore_signal(barrier, inc=1, device_id=device, device_id_type=MESH)

    for i in LINE:
        hello(z_peer(z, q, i))
    hello(q_peer(z, q, 2))
    hello(core_peer(s))
    for i in range(1, DP):
        hello(dp_peer(d, i))
    return lambda: pl.semaphore_wait(barrier, ZN + DP)


def received(ref, sem, device):
    push(ref, ref, sem, sem, device).wait_recv()


def sent(ref, sem, device):
    push(ref, ref, sem, sem, device).wait_send()


def each(low, high, f):
    def step(i, _):
        f(i)
        return 0

    lax.fori_loop(low, high, step, 0)


def whole_kernel(
    counts_in, w_in, b1_in, b2_in, cot_in, f1_in, f2_in, table_in,
    outg_ref, gf1_ref, gf2_ref, gwo_ref, gwv_ref,
    counts_ref, w_ref, table, b1_ref, b2_ref, w1_ref, w2_ref, v2_ref, v1_ref, tw_ref,
    own, wtt, wt_ref, lev_ref, cot_mid, cot_ref, f1_ref, f2_ref,
    levs, rows, crows, val, g1, g2, hid, gm, m1, m2, gh,
    tmp, inv, hat1, hat2, hatv, hath, hatg, hat_one_grad, gpb,
    out_s, out_mid, gf_s, gwp, gf_all, gw_in, gw_v, gw_g, flat, gf_o, gw_o,
    pre, loc, done, zr, xr, zs, gs, gr, fs, fr, cs, cr, os_, or_, hs, hr, ks, kr, ws, wr,
):
    s, d, z, q = place()
    m = s // 2
    core = lax.rem(s, 2)
    wait_barrier = greet(s, z, q, d)
    friend = dp_peer(d, 1)
    gw_all = (gw_v, gw_g)
    loads = [
        pltpu.make_async_copy(a, b, pre.at[i])
        for i, (a, b) in enumerate((
            (counts_in, counts_ref), (w_in, w_ref), (table_in, table),
            (b1_in, b1_ref), (b2_in, b2_ref),
        ))
    ]
    for load in loads:
        load.start()
    scale = 1.0 / math.sqrt(DP * BINS)
    base = s * CH

    def lanes(c):
        return slice(c * TILE, (c + 1) * TILE)

    def krows(c):
        return slice(c * SEQ, (c + 1) * SEQ)

    def put3(c, re, im):
        tmp[krows(c), 0:128] = re.astype(bf16)
        tmp[krows(c), 128:256] = im.astype(bf16)

    def forward(x_ref, dst):
        cr_ = tw_ref[0]
        ci_ = tw_ref[1]
        for p in range(CH // 2):
            x = x_ref[:, p * 256:(p + 1) * 256]
            part = dot(w1_ref[...], jnp.concatenate([x, x], axis=0))
            for h in range(2):
                re = part[0:32, lanes(h)]
                im = part[32:64, lanes(h)]
                put3(2 * p + h, re * cr_ - im * ci_, re * ci_ + im * cr_)
        dst[...] = dot(tmp[...], w2_ref[0:256, :]) + dot(tmp[...], w2_ref[256:512, :])

    def inverse(left, right, conj, emit):
        cr_ = tw_ref[0]
        ci_ = tw_ref[1]
        for c in range(CH):
            lr = left[krows(c), 0:128]
            li = left[krows(c), 128:256]
            rr = right[krows(c), 0:128]
            ri = right[krows(c), 128:256]
            if conj:
                put3(c, lr * rr + li * ri, lr * ri - li * rr)
            else:
                put3(c, lr * rr - li * ri, lr * ri + li * rr)
        inv[...] = dot(tmp[...], v2_ref[0:256, :]) + dot(tmp[...], v2_ref[256:512, :])
        for p in range(CH // 2):
            cols = []
            for h in range(2):
                c = 2 * p + h
                re = inv[krows(c), 0:128]
                im = inv[krows(c), 128:256]
                rh = (re * cr_ + im * ci_).astype(bf16)
                ih = (im * cr_ - re * ci_).astype(bf16)
                cols.append(jnp.concatenate([rh, ih, rh, ih], axis=0))
            res = dot(v1_ref[...], jnp.concatenate(cols, axis=1))
            for h in range(2):
                emit(2 * p + h, res[:, lanes(h)])

    def z_copy(i):
        return push(own, lev_ref.at[q, z], zs.at[0], zr.at[i], z_peer(z, q, i))

    def x_copy(i):
        slot = lev_ref.at[q, lax.rem(z - i + ZN, ZN)]
        return push(slot, slot, gs.at[0], xr.at[i], q_peer(z, q, 2))

    def g_copy(k, i):
        slot = lev_ref.at[lax.rem(q + k, GROUP), lax.rem(z - i + ZN, ZN)]
        return push(slot, slot, gs.at[0], gr.at[0], core_peer(s))

    def f_copy(i, src, dst, k):
        return push(src, dst.at[d], fs.at[k], fr.at[k], dp_peer(d, 2 * i))

    def fx_copy(src, dst, k):
        return push(src, dst.at[d], fs.at[k], fr.at[2 + k], {"dp": pair(d)})

    def fy_copy(i, dst, k):
        slot = dst.at[pair(d)]
        return push(slot, slot, fs.at[k], fr.at[k], dp_peer(d, 2 * i))

    def far_copy(i, src, mid, k, send, recv):
        to = lax.rem(m + i, SEQ // 2)
        return push(src.at[to], mid.at[m], send.at[k], recv.at[k], same_core(s, i))

    def near_copy(mid, dst, k, send, recv):
        return push(
            mid.at[:, 1 - core], dst.at[:, core], send.at[k], recv.at[k], core_peer(s)
        )

    def h_copy(which, i):
        to = lax.rem(d + i, DP)
        return push(
            gf_s.at[which, to], gf_all.at[which, d], hs.at[which], hr.at[which], dp_peer(d, i)
        )

    def part_rows(part):
        return slice(0, 16) if part == 0 else slice(16, 40)

    def k_copy(part, i):
        at = part_rows(part)
        return push(gwp.at[at], gw_in.at[d, at], ks.at[part], kr.at[part], dp_peer(d, i))

    def wz_copy(part, i):
        slot = gw_all[part].at[m, core]
        return push(slot, slot, ws.at[part], wr.at[part], same_core(s, i))

    def wg_copy(part):
        slot = gw_all[part].at[:, core]
        dst = gwv_ref.at[:, core] if part == 0 else slot
        return push(slot, dst, ws.at[2 + part], wr.at[2 + part], core_peer(s))

    loads[0].wait()
    levels = jnp.log1p(counts_ref[...].astype(f32)) - 3.0
    own[...] = levels.astype(bf16)
    lev_ref[q, z] = own[...]
    wait_barrier()
    for i in LINE:
        z_copy(i).start()

    x_copy(0).start()
    g_copy(0, 0).start()
    fx_copy(f1_in, f1_ref, 0).start()
    fx_copy(f2_in, f2_ref, 1).start()
    for i in FAR:
        if i % 2 == 0:
            far_copy(i, cot_in, cot_mid, 0, cs, cr).start()
    for i in range(1, DP // 2):
        f_copy(i, f1_in, f1_ref, 0).start()
        f_copy(i, f2_in, f2_ref, 1).start()
    keeps = [
        pltpu.make_async_copy(f1_in, f1_ref.at[d], loc.at[0]),
        pltpu.make_async_copy(f2_in, f2_ref.at[d], loc.at[1]),
        pltpu.make_async_copy(cot_in.at[m], cot_mid.at[m], loc.at[2]),
    ]
    for keep in keeps:
        keep.start()
    loads[1].wait()
    wtt[...] = w_ref[...].astype(f32).T
    for k in range(3):
        at = pl.multiple_of(k * D + s * CH, 8)
        wt_ref[k * CH:(k + 1) * CH, :] = wtt[pl.ds(at, CH), :].astype(bf16)
    levs[EVENTS:, :] = jnp.zeros((TILE - EVENTS, BINS), bf16)
    for load in loads[2:]:
        load.wait()
    for at, ref in ((0, w2_ref), (256, v2_ref)):
        hi, lo = split(table[at:at + 256, :])
        ref[0:256, :] = hi
        ref[256:512, :] = lo
    hi, lo = split(table[512:576, 0:32])
    w1_ref[...] = jnp.concatenate([hi, lo], axis=1)
    hi, lo = split(table[576:608, 0:64])
    v1_ref[...] = jnp.concatenate([hi, lo], axis=1)
    tw_ref[0] = table[608:640, 0:128]
    tw_ref[1] = table[608:640, 128:256]

    x_copy(0).wait_recv()
    g_copy(2, 0).start()
    for i in FAR:
        if i % 2 == 1:
            far_copy(i, cot_in, cot_mid, 0, cs, cr).start()
    for i in LINE:
        z_copy(i).wait_recv()
        x_copy(i).start()
        g_copy(0, i).start()
    for ref, k in ((f1_ref, 0), (f2_ref, 1)):
        received(ref.at[0], fr.at[2 + k], friend)
        for j in range(1, DP // 2):
            fy_copy(j, ref, k).start()
    for i in LINE:
        x_copy(i).wait_recv()
        g_copy(2, i).start()

    def load_filter(ref, dst):
        for e in range(DP):
            for p in range(BINS // DP // TILE):
                a = e * (BINS // DP // TILE) + p
                crows[a * CH:(a + 1) * CH, :] = ref[e, :, p * TILE:(p + 1) * TILE].astype(f32)
        for c in range(CH):
            hid[:, lanes(c)] = crows[pl.ds(c, SEQ, stride=CH), :].astype(bf16)
        forward(hid, dst)

    keeps[0].wait()
    received(f1_ref.at[0:DP - 2], fr.at[0], friend)
    load_filter(f1_ref, hat1)
    keeps[1].wait()
    received(f2_ref.at[0:DP - 2], fr.at[1], friend)
    load_filter(f2_ref, hat2)

    received(lev_ref.at[0:2], gr.at[0], friend)
    for a in range(SEQ):
        levs[0:EVENTS, a * TILE:(a + 1) * TILE] = lev_ref[a % GROUP, a // GROUP]
    for p in range(SEQ // 2):
        proj = dot(wt_ref[...], levs[0:EVENTS, p * 256:(p + 1) * 256])
        for h in range(2):
            a = 2 * p + h
            rows[a * COLS:(a + 1) * COLS, :] = proj[:, lanes(h)]
    for c in range(CH):
        val[:, lanes(c)] = rows[pl.ds(c, SEQ, stride=COLS), :].astype(bf16)
        g1[:, lanes(c)] = rows[pl.ds(CH + c, SEQ, stride=COLS), :].astype(bf16)
        g2[:, lanes(c)] = rows[pl.ds(2 * CH + c, SEQ, stride=COLS), :].astype(bf16)
    keeps[2].wait()
    received(cot_mid.at[0:SEQ // 2 - 1], cr.at[0], friend)
    near_copy(cot_mid, cot_ref, 1, cs, cr).start()
    keep_cot = pltpu.make_async_copy(cot_mid.at[:, core], cot_ref.at[:, core], loc.at[3])
    keep_cot.start()
    forward(val, hatv)

    def emit_one(c, conv):
        mixed = rnd(conv) + b1_ref[base + c] * val[:, lanes(c)].astype(f32)
        m1[:, lanes(c)] = mixed
        hid[:, lanes(c)] = (g1[:, lanes(c)].astype(f32) * mixed).astype(bf16)

    inverse(hat1, hatv, False, emit_one)
    forward(hid, hath)

    def emit_two(c, conv):
        mixed = rnd(conv) + b2_ref[base + c] * hid[:, lanes(c)].astype(f32)
        m2[:, lanes(c)] = mixed
        crows[pl.ds(c, SEQ, stride=CH), :] = g2[:, lanes(c)].astype(f32) * mixed

    inverse(hat2, hath, False, emit_two)
    for a in range(SEQ):
        out_s[a // 2, a % 2] = crows[a * CH:(a + 1) * CH, :].astype(bf16)
    for i in FAR:
        far_copy(i, out_s, out_mid, 0, os_, or_).start()
    keep_out = pltpu.make_async_copy(out_s.at[m], out_mid.at[m], loc.at[4])
    keep_out.start()

    keep_cot.wait()
    received(cot_ref.at[:, 0], cr.at[1], friend)
    for a in range(SEQ):
        crows[a * CH:(a + 1) * CH, :] = cot_ref[a // 2, a % 2].astype(f32)
    for c in range(CH):
        up = crows[pl.ds(c, SEQ, stride=CH), :] * scale
        rows[pl.ds(2 * CH + c, SEQ, stride=COLS), :] = up * m2[:, lanes(c)]
        gm[:, lanes(c)] = (up * g2[:, lanes(c)].astype(f32)).astype(bf16)

    def bias_sums(x_ref, y_ref):
        parts = []
        for c in range(CH):
            t = x_ref[:, lanes(c)].astype(f32) * y_ref[:, lanes(c)].astype(f32)
            parts.append(jnp.sum(t, axis=0, keepdims=True))
        return jnp.sum(jnp.concatenate(parts, axis=0), axis=1, keepdims=True)

    def weight_rows(part, sums):
        low, high = ((0, CH), (CH, COLS))[part]
        for a in range(SEQ):
            gpb[low:high, a * TILE:(a + 1) * TILE] = rows[
                a * COLS + low:a * COLS + high, :
            ].astype(bf16)
        weight = lax.dot_general(
            gpb[low:high, :], levs[...], (((1,), (1,)), ((), ())), preferred_element_type=f32
        )
        packed = [
            weight[r:r + 8] + pltpu.roll(weight[r + 8:r + 16], EVENTS, 1)
            for r in range(0, high - low - 8, 16)
        ]
        if part == 0:
            lane = lax.broadcasted_iota(jnp.int32, (8, TILE), 1)
            last = weight[16:24]
            for k, total in enumerate(sums):
                for r in range(3):
                    last = jnp.where(lane == EVENTS + 3 * k + r, total[8 * r:8 * r + 8], last)
            packed.append(last)
        packed = jnp.concatenate(packed, axis=0)
        gwp[part_rows(part), :] = packed
        gw_in[d, part_rows(part), :] = packed

    def total_rows(part):
        total = gw_in[0, part_rows(part), :]
        for k in range(1, DP):
            total = total + gw_in[k, part_rows(part), :]
        gw_all[part][m, core] = total.astype(bf16)

    def emit_gf(which):
        def emit(c, conv):
            gf_s[which, c // 3, :, (c % 3) * TILE:(c % 3 + 1) * TILE] = conv.astype(bf16)
        return emit

    gives = []

    def give(src, dst, k):
        copy = pltpu.make_async_copy(src, dst, done.at[k])
        copy.start()
        gives.append(copy)

    def finish_filter(which, dst):
        received(gf_all.at[which, 0:DP - 1], hr.at[which], friend)
        total = gf_all[which, 0].astype(f32)
        for k in range(1, DP):
            total = total + gf_all[which, k].astype(f32)
        for c in range(3):
            for a in range(SEQ):
                flat[c:c + 1, a * TILE:(a + 1) * TILE] = total[a:a + 1, lanes(c)]
        gf_o[which] = flat[0:3, :].astype(bf16)
        give(gf_o.at[which], dst, which)

    forward(gm, hatg)
    sum_two = bias_sums(gm, hid)

    def emit_carried_two(c, conv):
        ghid = b2_ref[base + c] * gm[:, lanes(c)].astype(f32) + rnd(conv)
        gh[:, lanes(c)] = (ghid * g1[:, lanes(c)].astype(f32)).astype(bf16)
        rows[pl.ds(CH + c, SEQ, stride=COLS), :] = ghid * m1[:, lanes(c)]

    inverse(hat2, hatg, True, emit_carried_two)
    weight_rows(1, ())
    for i in range(1, DP):
        k_copy(1, i).start()

    forward(gh, hat_one_grad)
    sum_one = bias_sums(gh, val)

    def emit_carried_one(c, conv):
        rows[pl.ds(c, SEQ, stride=COLS), :] = (
            b1_ref[base + c] * gh[:, lanes(c)].astype(f32) + rnd(conv)
        )

    inverse(hat1, hat_one_grad, True, emit_carried_one)
    weight_rows(0, (sum_one, sum_two))
    for i in range(1, DP):
        k_copy(0, i).start()

    inverse(hath, hatg, True, emit_gf(1))
    gf_all[1, d] = gf_s[1, d]
    for i in range(1, DP):
        h_copy(1, i).start()

    received(gw_in.at[0:DP - 1, part_rows(1)], kr.at[1], friend)
    total_rows(1)
    for i in FAR:
        wz_copy(1, i).start()
    inverse(hatv, hat_one_grad, True, emit_gf(0))
    gf_all[0, d] = gf_s[0, d]
    for i in range(1, DP):
        h_copy(0, i).start()

    keep_out.wait()
    received(out_mid.at[0:SEQ // 2 - 1], or_.at[0], friend)
    near_copy(out_mid, outg_ref, 1, os_, or_).start()
    keep_plane = pltpu.make_async_copy(out_mid.at[:, core], outg_ref.at[:, core], loc.at[5])
    keep_plane.start()
    received(gw_in.at[0:DP - 1, part_rows(0)], kr.at[0], friend)
    total_rows(0)
    for i in FAR:
        wz_copy(0, i).start()

    def turn(k):
        block = []
        for n in range(SEQ):
            b = gw_g[n // 2, n % 2].astype(f32)
            tiles = [b[r:r + 8] for r in range(0, 24, 8)]
            if k == 1:
                block += [tiles[0], pltpu.roll(tiles[0], EVENTS, 1), tiles[1]]
            else:
                block += [
                    pltpu.roll(tiles[1], EVENTS, 1), tiles[2], pltpu.roll(tiles[2], EVENTS, 1)
                ]
        for p in range(D // TILE):
            turned = jnp.concatenate(block[16 * p:16 * p + 16], axis=0).T
            at = (k - 1) * D + p * TILE
            gw_o[:, at:at + TILE] = turned[0:EVENTS, :]

    def pass_weights(part):
        received(gw_all[part].at[0:SEQ // 2 - 1, 0], wr.at[part], friend)
        wg_copy(part).start()

    pass_weights(1)
    finish_filter(1, gf2_ref)
    received(gw_all[1].at[:, 0], wr.at[3], friend)
    turn(1)
    turn(2)
    give(gw_o, gwo_ref, 2)
    pass_weights(0)
    give(gw_v.at[:, core], gwv_ref.at[:, core], 3)
    finish_filter(0, gf1_ref)
    received(gw_v.at[:, 0], wr.at[2], friend)
    keep_plane.wait()
    received(outg_ref.at[:, 0], or_.at[1], friend)
    sent(lev_ref.at[0, 0:ZN - 1], zs.at[0], friend)
    sent(lev_ref.at[0:GROUP - 1], gs.at[0], friend)
    sent(f1_ref.at[0:DP - 1], fs.at[0], friend)
    sent(f2_ref.at[0:DP - 1], fs.at[1], friend)
    sent(cot_mid.at[0:SEQ // 2 - 1], cs.at[0], friend)
    sent(cot_ref.at[:, 0], cs.at[1], friend)
    sent(out_mid.at[0:SEQ // 2 - 1], os_.at[0], friend)
    sent(outg_ref.at[:, 0], os_.at[1], friend)
    for part in range(2):
        sent(gf_all.at[part, 0:DP - 1], hs.at[part], friend)
        sent(gw_in.at[0:DP - 1, part_rows(part)], ks.at[part], friend)
        sent(gw_all[part].at[0:SEQ // 2 - 1, 0], ws.at[part], friend)
        sent(gw_all[part].at[:, 0], ws.at[2 + part], friend)
    for copy in gives:
        copy.wait()


def whole(counts, w_in, b1, b2, cot, f1, f2):
    dma = pltpu.SemaphoreType.DMA
    vm = pltpu.VMEM
    spec = (SEQ * CH, 2 * TILE)
    return pl.pallas_call(
        whole_kernel,
        out_shape=(
            jax.ShapeDtypeStruct((SEQ // 2, 2, CH, TILE), bf16),
            jax.ShapeDtypeStruct((3, BINS), bf16),
            jax.ShapeDtypeStruct((3, BINS), bf16),
            jax.ShapeDtypeStruct((EVENTS, 2 * D), f32),
            jax.ShapeDtypeStruct((SEQ // 2, 2, 16, TILE), bf16),
        ),
        in_specs=[ANY] * 8,
        out_specs=(ANY,) * 5,
        scratch_shapes=[
            vm((EVENTS, TILE), jnp.int32),
            vm((EVENTS, 3 * D), bf16),
            vm((640, 2 * TILE), f32),
            pltpu.SMEM((D,), f32),
            pltpu.SMEM((D,), f32),
            vm((2 * SEQ, 2 * SEQ), bf16),
            vm((4 * TILE, 2 * TILE), bf16),
            vm((4 * TILE, 2 * TILE), bf16),
            vm((SEQ, 4 * SEQ), bf16),
            vm((2, SEQ, TILE), f32),
            vm((EVENTS, TILE), bf16),
            vm((3 * D, EVENTS), f32),
            vm((COLS, EVENTS), bf16),
            vm((GROUP, ZN, EVENTS, TILE), bf16),
            vm((SEQ // 2, 2, CH, TILE), bf16),
            vm((SEQ // 2, 2, CH, TILE), bf16),
            vm((DP, CH, BINS // DP), bf16),
            vm((DP, CH, BINS // DP), bf16),
            vm((TILE, BINS), bf16),
            vm((SEQ * COLS, TILE), f32),
            vm((SEQ * CH, TILE), f32),
            vm((SEQ, LANES), bf16),
            vm((SEQ, LANES), bf16),
            vm((SEQ, LANES), bf16),
            vm((SEQ, LANES), bf16),
            vm((SEQ, LANES), bf16),
            vm((SEQ, LANES), f32),
            vm((SEQ, LANES), f32),
            vm((SEQ, LANES), bf16),
            vm((SEQ * CH, 2 * TILE), bf16),
            vm(spec, f32),
            vm(spec, f32),
            vm(spec, f32),
            vm(spec, f32),
            vm(spec, f32),
            vm(spec, f32),
            vm(spec, f32),
            vm((COLS, BINS), bf16),
            vm((SEQ // 2, 2, CH, TILE), bf16),
            vm((SEQ // 2, 2, CH, TILE), bf16),
            vm((2, DP, SEQ, 3 * TILE), bf16),
            vm((40, TILE), f32),
            vm((2, DP, SEQ, 3 * TILE), bf16),
            vm((DP, 40, TILE), f32),
            vm((SEQ // 2, 2, 16, TILE), bf16),
            vm((SEQ // 2, 2, 24, TILE), bf16),
            vm((8, BINS), f32),
            vm((2, 3, BINS), bf16),
            vm((EVENTS, 2 * D), f32),
            dma((5,)),
            dma((6,)),
            dma((6,)),
            dma((8,)),
            dma((8,)),
            dma((1,)),
            dma((1,)),
            dma((1,)),
            dma((2,)),
            dma((4,)),
            dma((2,)),
            dma((2,)),
            dma((2,)),
            dma((2,)),
            dma((2,)),
            dma((2,)),
            dma((2,)),
            dma((2,)),
            dma((4,)),
            dma((4,)),
        ],
        compiler_params=pltpu.CompilerParams(
            collective_id=0, has_side_effects=True, vmem_limit_bytes=LIMIT
        ),
        name="whole",
    )(counts, w_in, b1, b2, cot, f1, f2, tables())


def finish_kernel(
    out_in, gf1_in, gf2_in, gates_in, value_in,
    out_ref, gf1_ref, gf2_ref, gw_ref, gb1_ref, gb2_ref,
):
    low = lax.broadcasted_iota(jnp.int32, (8, TILE), 1) < EVENTS
    block = []
    for n in range(SEQ):
        b = value_in[n // 2, n % 2].astype(f32)
        first, last = b[0:8], b[8:16]
        block.append(jnp.where(low, first, last))
        block.append(
            jnp.where(low, pltpu.roll(first, EVENTS, 1), pltpu.roll(last, TILE - 1, 1))
        )
        block.append(jnp.where(low, last, pltpu.roll(last, TILE - 2, 1)))
    for p in range(D // TILE):
        turned = jnp.concatenate(block[16 * p:16 * p + 16], axis=0).T
        at = slice(p * TILE, (p + 1) * TILE)
        gw_ref[:, at] = turned[0:EVENTS, :]
        gb1_ref[at] = turned[EVENTS]
        gb2_ref[at] = turned[EVENTS + 3]
    gw_ref[:, D:] = gates_in[...]
    out_ref[...] = out_in[...]
    gf1_ref[...] = gf1_in[...]
    gf2_ref[...] = gf2_in[...]


def finish(out, gf1, gf2, gates, value):
    def like(x):
        return jax.ShapeDtypeStruct(x.shape, x.dtype)

    flat = jax.ShapeDtypeStruct((D,), f32)
    return pl.pallas_call(
        finish_kernel,
        out_shape=(
            like(out), like(gf1), like(gf2), jax.ShapeDtypeStruct((EVENTS, 3 * D), f32), flat, flat
        ),
        in_specs=[VMEM] * 5,
        out_specs=(VMEM,) * 6,
        compiler_params=pltpu.CompilerParams(vmem_limit_bytes=LIMIT),
        name="finish",
    )(out, gf1, gf2, gates, value)


def body(counts, w_in, bias_one, bias_two, filter_one, filter_two, cotangent):
    out, gf1, gf2, gates, value = whole(
        counts[0].T, w_in, bias_one, bias_two, cotangent.reshape(SEQ // 2, 2, CH, TILE),
        filter_one, filter_two,
    )
    out, gf1, gf2, gw, gb1, gb2 = finish(out.reshape(1, D, TILE), gf1, gf2, gates, value)
    return out, gw, gb1, gb2, gf1, gf2


def solution(mesh):
    return jax.shard_map(
        body,
        mesh=mesh,
        in_specs=(
            P("dp", "seq", None),
            P(),
            P(),
            P(),
            P("seq", "dp"),
            P("seq", "dp"),
            P("dp", None, "seq"),
        ),
        out_specs=(
            P("dp", None, "seq"),
            P(),
            P(),
            P(),
            P(("seq", "dp"), None),
            P(("seq", "dp"), None),
        ),
        check_vma=False,
    )
```

```python
import functools
import math

import jax
import jax.numpy as jnp
import numpy as np
from jax import lax
from jax.experimental import pallas as pl
from jax.experimental.pallas import tpu as pltpu
from jax.sharding import PartitionSpec as P

SEQ = 32
DP = 8
ZN = 8
GROUP = 4
TILE = 128
EVENTS = 64
CH = 24
D = SEQ * CH
BINS = SEQ * TILE
COLS = 3 * CH
LANES = CH * TILE
f32 = jnp.float32
bf16 = jnp.bfloat16
MESH = pl.DeviceIdType.MESH
VMEM = pl.BlockSpec(memory_space=pltpu.VMEM)
SMEM = pl.BlockSpec(memory_space=pltpu.SMEM)
ANY = pl.BlockSpec(memory_space=pl.ANY)
LIMIT = 56 * 1024 * 1024
LINE = (4, 3, 5, 2, 6, 1, 7)
FAR = (8, 7, 9, 6, 10, 5, 11, 4, 12, 3, 13, 2, 14, 1, 15)


def tables():
    a = np.arange(SEQ)
    j = np.arange(TILE)
    k1 = np.arange(SEQ) + 0.25
    k2 = np.arange(TILE)
    first = np.exp(-2j * np.pi * np.outer(k1, a) / SEQ)
    turn = np.exp(-2j * np.pi * np.outer(k1, j) / BINS)
    second = np.exp(-2j * np.pi * np.outer(j, k2) / TILE)
    w1 = np.concatenate([first.real, first.imag], axis=0)
    w2 = np.block([[second.real, second.imag], [-second.imag, second.real]])
    inv2 = np.conj(second).T
    v2 = np.block([[inv2.real, inv2.imag], [-inv2.imag, inv2.real]])
    last = np.conj(first).T / BINS
    v1 = np.concatenate([last.real, -last.imag], axis=1)

    table = np.zeros((640, 2 * TILE), np.float32)
    table[0:256] = w2
    table[256:512] = v2
    table[512:576, 0:32] = w1
    table[576:608, 0:64] = v1
    table[608:640, 0:128] = turn.real
    table[608:640, 128:256] = turn.imag
    return table


def dot(x, y):
    return jnp.dot(x, y, preferred_element_type=f32)


def split(x):
    hi = x.astype(bf16)
    lo = (x - hi.astype(f32)).astype(bf16)
    return hi, lo


def rnd(x):
    return x.astype(bf16).astype(f32)


def place():
    s = lax.axis_index("seq")
    d = lax.axis_index("dp")
    return s, d, s // GROUP, lax.rem(s, GROUP)


def dp_peer(d, i):
    return {"dp": lax.rem(d + i, DP)}


def z_peer(z, q, i):
    return {"seq": lax.rem(z + i, ZN) * GROUP + q}


def q_peer(z, q, r):
    return {"seq": z * GROUP + lax.rem(q + r, GROUP)}


def push(src, dst, send, recv, device):
    return pltpu.make_async_remote_copy(
        src_ref=src, dst_ref=dst, send_sem=send, recv_sem=recv,
        device_id=device, device_id_type=MESH,
    )


def same_core(s, i):
    return {"seq": lax.rem(s + 2 * i, SEQ)}


def core_peer(s):
    return {"seq": s + 1 - 2 * lax.rem(s, 2)}


def pair(d):
    return d + 1 - 2 * lax.rem(d, 2)


def greet(s, z, q, d):
    barrier = pltpu.get_barrier_semaphore()

    def hello(device):
        pl.semaphore_signal(barrier, inc=1, device_id=device, device_id_type=MESH)

    for i in LINE:
        hello(z_peer(z, q, i))
    hello(q_peer(z, q, 2))
    hello(core_peer(s))
    for i in range(1, DP):
        hello(dp_peer(d, i))
    return lambda: pl.semaphore_wait(barrier, ZN + DP)


def received(ref, sem, device):
    push(ref, ref, sem, sem, device).wait_recv()


def sent(ref, sem, device):
    push(ref, ref, sem, sem, device).wait_send()


def each(low, high, f):
    def step(i, _):
        f(i)
        return 0

    lax.fori_loop(low, high, step, 0)


def whole_kernel(
    counts_in, w_in, b1_in, b2_in, cot_in, f1_in, f2_in, table_in,
    outg_ref, gf1_ref, gf2_ref, gwo_ref, gwv_ref,
    counts_ref, w_ref, table, b1_ref, b2_ref, w1_ref, w2_ref, v2_ref, v1_ref, tw_ref,
    own, wtt, wt_ref, lev_ref, cot_mid, cot_ref, f1_ref, f2_ref,
    levs, rows, crows, val, g1, g2, hid, gm, m1, m2, gh,
    tmp, inv, hat1, hat2, hatv, hath, hatg, hat_one_grad, gpb,
    out_s, out_mid, gf_s, gwp, gf_all, gw_in, gw_v, gw_g, flat, gf_o, gw_o,
    pre, loc, done, zr, xr, zs, gs, gr, fs, fr, cs, cr, os_, or_, hs, hr, ks, kr, ws, wr,
):
    s, d, z, q = place()
    m = s // 2
    core = lax.rem(s, 2)
    wait_barrier = greet(s, z, q, d)
    friend = dp_peer(d, 1)
    gw_all = (gw_v, gw_g)
    loads = [
        pltpu.make_async_copy(a, b, pre.at[i])
        for i, (a, b) in enumerate((
            (counts_in, counts_ref), (w_in, w_ref), (table_in, table),
            (b1_in, b1_ref), (b2_in, b2_ref),
        ))
    ]
    for load in loads:
        load.start()
    scale = 1.0 / math.sqrt(DP * BINS)
    base = s * CH

    def lanes(c):
        return slice(c * TILE, (c + 1) * TILE)

    def krows(c):
        return slice(c * SEQ, (c + 1) * SEQ)

    def put3(c, re, im):
        tmp[krows(c), 0:128] = re.astype(bf16)
        tmp[krows(c), 128:256] = im.astype(bf16)

    def forward(x_ref, dst):
        cr_ = tw_ref[0]
        ci_ = tw_ref[1]
        for p in range(CH // 2):
            x = x_ref[:, p * 256:(p + 1) * 256]
            part = dot(w1_ref[...], jnp.concatenate([x, x], axis=0))
            for h in range(2):
                re = part[0:32, lanes(h)]
                im = part[32:64, lanes(h)]
                put3(2 * p + h, re * cr_ - im * ci_, re * ci_ + im * cr_)
        dst[...] = dot(tmp[...], w2_ref[0:256, :]) + dot(tmp[...], w2_ref[256:512, :])

    def inverse(left, right, conj, emit):
        cr_ = tw_ref[0]
        ci_ = tw_ref[1]
        for c in range(CH):
            lr = left[krows(c), 0:128]
            li = left[krows(c), 128:256]
            rr = right[krows(c), 0:128]
            ri = right[krows(c), 128:256]
            if conj:
                put3(c, lr * rr + li * ri, lr * ri - li * rr)
            else:
                put3(c, lr * rr - li * ri, lr * ri + li * rr)
        inv[...] = dot(tmp[...], v2_ref[0:256, :]) + dot(tmp[...], v2_ref[256:512, :])
        for p in range(CH // 2):
            cols = []
            for h in range(2):
                c = 2 * p + h
                re = inv[krows(c), 0:128]
                im = inv[krows(c), 128:256]
                rh = (re * cr_ + im * ci_).astype(bf16)
                ih = (im * cr_ - re * ci_).astype(bf16)
                cols.append(jnp.concatenate([rh, ih, rh, ih], axis=0))
            res = dot(v1_ref[...], jnp.concatenate(cols, axis=1))
            for h in range(2):
                emit(2 * p + h, res[:, lanes(h)])

    def z_copy(i):
        return push(own, lev_ref.at[q, z], zs.at[0], zr.at[i], z_peer(z, q, i))

    def x_copy(i):
        slot = lev_ref.at[q, lax.rem(z - i + ZN, ZN)]
        return push(slot, slot, gs.at[0], xr.at[i], q_peer(z, q, 2))

    def g_copy(k, i):
        slot = lev_ref.at[lax.rem(q + k, GROUP), lax.rem(z - i + ZN, ZN)]
        return push(slot, slot, gs.at[0], gr.at[0], core_peer(s))

    def f_copy(i, src, dst, k):
        return push(src, dst.at[d], fs.at[k], fr.at[k], dp_peer(d, 2 * i))

    def fx_copy(src, dst, k):
        return push(src, dst.at[d], fs.at[k], fr.at[2 + k], {"dp": pair(d)})

    def fy_copy(i, dst, k):
        slot = dst.at[pair(d)]
        return push(slot, slot, fs.at[k], fr.at[k], dp_peer(d, 2 * i))

    def far_copy(i, src, mid, k, send, recv):
        to = lax.rem(m + i, SEQ // 2)
        return push(src.at[to], mid.at[m], send.at[k], recv.at[k], same_core(s, i))

    def near_copy(mid, dst, k, send, recv):
        return push(
            mid.at[:, 1 - core], dst.at[:, core], send.at[k], recv.at[k], core_peer(s)
        )

    def h_copy(which, i):
        to = lax.rem(d + i, DP)
        return push(
            gf_s.at[which, to], gf_all.at[which, d], hs.at[which], hr.at[which], dp_peer(d, i)
        )

    def part_rows(part):
        return slice(0, 16) if part == 0 else slice(16, 40)

    def k_copy(part, i):
        at = part_rows(part)
        return push(gwp.at[at], gw_in.at[d, at], ks.at[part], kr.at[part], dp_peer(d, i))

    def wz_copy(part, i):
        slot = gw_all[part].at[m, core]
        return push(slot, slot, ws.at[part], wr.at[part], same_core(s, i))

    def wg_copy(part):
        slot = gw_all[part].at[:, core]
        dst = gwv_ref.at[:, core] if part == 0 else slot
        return push(slot, dst, ws.at[2 + part], wr.at[2 + part], core_peer(s))

    loads[0].wait()
    levels = jnp.log1p(counts_ref[...].astype(f32)) - 3.0
    own[...] = levels.astype(bf16)
    lev_ref[q, z] = own[...]
    wait_barrier()
    for i in LINE:
        z_copy(i).start()

    x_copy(0).start()
    g_copy(0, 0).start()
    fx_copy(f1_in, f1_ref, 0).start()
    fx_copy(f2_in, f2_ref, 1).start()
    for i in FAR:
        if i % 2 == 0:
            far_copy(i, cot_in, cot_mid, 0, cs, cr).start()
    for i in range(1, DP // 2):
        f_copy(i, f1_in, f1_ref, 0).start()
        f_copy(i, f2_in, f2_ref, 1).start()
    keeps = [
        pltpu.make_async_copy(f1_in, f1_ref.at[d], loc.at[0]),
        pltpu.make_async_copy(f2_in, f2_ref.at[d], loc.at[1]),
        pltpu.make_async_copy(cot_in.at[m], cot_mid.at[m], loc.at[2]),
    ]
    for keep in keeps:
        keep.start()
    loads[1].wait()
    wtt[...] = w_ref[...].astype(f32).T
    for k in range(3):
        at = pl.multiple_of(k * D + s * CH, 8)
        wt_ref[k * CH:(k + 1) * CH, :] = wtt[pl.ds(at, CH), :].astype(bf16)
    levs[EVENTS:, :] = jnp.zeros((TILE - EVENTS, BINS), bf16)
    for load in loads[2:]:
        load.wait()
    for at, ref in ((0, w2_ref), (256, v2_ref)):
        hi, lo = split(table[at:at + 256, :])
        ref[0:256, :] = hi
        ref[256:512, :] = lo
    hi, lo = split(table[512:576, 0:32])
    w1_ref[...] = jnp.concatenate([hi, lo], axis=1)
    hi, lo = split(table[576:608, 0:64])
    v1_ref[...] = jnp.concatenate([hi, lo], axis=1)
    tw_ref[0] = table[608:640, 0:128]
    tw_ref[1] = table[608:640, 128:256]

    x_copy(0).wait_recv()
    g_copy(2, 0).start()
    for i in FAR:
        if i % 2 == 1:
            far_copy(i, cot_in, cot_mid, 0, cs, cr).start()
    for i in LINE:
        z_copy(i).wait_recv()
        x_copy(i).start()
        g_copy(0, i).start()
    for ref, k in ((f1_ref, 0), (f2_ref, 1)):
        received(ref.at[0], fr.at[2 + k], friend)
        for j in range(1, DP // 2):
            fy_copy(j, ref, k).start()
    for i in LINE:
        x_copy(i).wait_recv()
        g_copy(2, i).start()

    def load_filter(ref, dst):
        for e in range(DP):
            for p in range(BINS // DP // TILE):
                a = e * (BINS // DP // TILE) + p
                crows[a * CH:(a + 1) * CH, :] = ref[e, :, p * TILE:(p + 1) * TILE].astype(f32)
        for c in range(CH):
            hid[:, lanes(c)] = crows[pl.ds(c, SEQ, stride=CH), :].astype(bf16)
        forward(hid, dst)

    keeps[0].wait()
    received(f1_ref.at[0:DP - 2], fr.at[0], friend)
    load_filter(f1_ref, hat1)
    keeps[1].wait()
    received(f2_ref.at[0:DP - 2], fr.at[1], friend)
    load_filter(f2_ref, hat2)

    received(lev_ref.at[0:2], gr.at[0], friend)
    for a in range(SEQ):
        levs[0:EVENTS, a * TILE:(a + 1) * TILE] = lev_ref[a % GROUP, a // GROUP]
    for p in range(SEQ // 2):
        proj = dot(wt_ref[...], levs[0:EVENTS, p * 256:(p + 1) * 256])
        for h in range(2):
            a = 2 * p + h
            rows[a * COLS:(a + 1) * COLS, :] = proj[:, lanes(h)]
    for c in range(CH):
        val[:, lanes(c)] = rows[pl.ds(c, SEQ, stride=COLS), :].astype(bf16)
        g1[:, lanes(c)] = rows[pl.ds(CH + c, SEQ, stride=COLS), :].astype(bf16)
        g2[:, lanes(c)] = rows[pl.ds(2 * CH + c, SEQ, stride=COLS), :].astype(bf16)
    keeps[2].wait()
    received(cot_mid.at[0:SEQ // 2 - 1], cr.at[0], friend)
    near_copy(cot_mid, cot_ref, 1, cs, cr).start()
    keep_cot = pltpu.make_async_copy(cot_mid.at[:, core], cot_ref.at[:, core], loc.at[3])
    keep_cot.start()
    forward(val, hatv)

    def emit_one(c, conv):
        mixed = rnd(conv) + b1_ref[base + c] * val[:, lanes(c)].astype(f32)
        m1[:, lanes(c)] = mixed
        hid[:, lanes(c)] = (g1[:, lanes(c)].astype(f32) * mixed).astype(bf16)

    inverse(hat1, hatv, False, emit_one)
    forward(hid, hath)

    def emit_two(c, conv):
        mixed = rnd(conv) + b2_ref[base + c] * hid[:, lanes(c)].astype(f32)
        m2[:, lanes(c)] = mixed
        crows[pl.ds(c, SEQ, stride=CH), :] = g2[:, lanes(c)].astype(f32) * mixed

    inverse(hat2, hath, False, emit_two)
    for a in range(SEQ):
        out_s[a // 2, a % 2] = crows[a * CH:(a + 1) * CH, :].astype(bf16)
    for i in FAR:
        far_copy(i, out_s, out_mid, 0, os_, or_).start()
    keep_out = pltpu.make_async_copy(out_s.at[m], out_mid.at[m], loc.at[4])
    keep_out.start()

    keep_cot.wait()
    received(cot_ref.at[:, 0], cr.at[1], friend)
    for a in range(SEQ):
        crows[a * CH:(a + 1) * CH, :] = cot_ref[a // 2, a % 2].astype(f32)
    for c in range(CH):
        up = crows[pl.ds(c, SEQ, stride=CH), :] * scale
        rows[pl.ds(2 * CH + c, SEQ, stride=COLS), :] = up * m2[:, lanes(c)]
        gm[:, lanes(c)] = (up * g2[:, lanes(c)].astype(f32)).astype(bf16)

    def bias_sums(x_ref, y_ref):
        parts = []
        for c in range(CH):
            t = x_ref[:, lanes(c)].astype(f32) * y_ref[:, lanes(c)].astype(f32)
            parts.append(jnp.sum(t, axis=0, keepdims=True))
        return jnp.sum(jnp.concatenate(parts, axis=0), axis=1, keepdims=True)

    def weight_rows(part, sums):
        low, high = ((0, CH), (CH, COLS))[part]
        for a in range(SEQ):
            gpb[low:high, a * TILE:(a + 1) * TILE] = rows[
                a * COLS + low:a * COLS + high, :
            ].astype(bf16)
        weight = lax.dot_general(
            gpb[low:high, :], levs[...], (((1,), (1,)), ((), ())), preferred_element_type=f32
        )
        packed = [
            weight[r:r + 8] + pltpu.roll(weight[r + 8:r + 16], EVENTS, 1)
            for r in range(0, high - low - 8, 16)
        ]
        if part == 0:
            lane = lax.broadcasted_iota(jnp.int32, (8, TILE), 1)
            last = weight[16:24]
            for k, total in enumerate(sums):
                for r in range(3):
                    last = jnp.where(lane == EVENTS + 3 * k + r, total[8 * r:8 * r + 8], last)
            packed.append(last)
        packed = jnp.concatenate(packed, axis=0)
        gwp[part_rows(part), :] = packed
        gw_in[d, part_rows(part), :] = packed

    def total_rows(part):
        total = gw_in[0, part_rows(part), :]
        for k in range(1, DP):
            total = total + gw_in[k, part_rows(part), :]
        gw_all[part][m, core] = total.astype(bf16)

    def emit_gf(which):
        def emit(c, conv):
            gf_s[which, c // 3, :, (c % 3) * TILE:(c % 3 + 1) * TILE] = conv.astype(bf16)
        return emit

    gives = []

    def give(src, dst, k):
        copy = pltpu.make_async_copy(src, dst, done.at[k])
        copy.start()
        gives.append(copy)

    def finish_filter(which, dst):
        received(gf_all.at[which, 0:DP - 1], hr.at[which], friend)
        total = gf_all[which, 0].astype(f32)
        for k in range(1, DP):
            total = total + gf_all[which, k].astype(f32)
        for c in range(3):
            for a in range(SEQ):
                flat[c:c + 1, a * TILE:(a + 1) * TILE] = total[a:a + 1, lanes(c)]
        gf_o[which] = flat[0:3, :].astype(bf16)
        give(gf_o.at[which], dst, which)

    forward(gm, hatg)
    sum_two = bias_sums(gm, hid)

    def emit_carried_two(c, conv):
        ghid = b2_ref[base + c] * gm[:, lanes(c)].astype(f32) + rnd(conv)
        gh[:, lanes(c)] = (ghid * g1[:, lanes(c)].astype(f32)).astype(bf16)
        rows[pl.ds(CH + c, SEQ, stride=COLS), :] = ghid * m1[:, lanes(c)]

    inverse(hat2, hatg, True, emit_carried_two)
    weight_rows(1, ())
    for i in range(1, DP):
        k_copy(1, i).start()

    forward(gh, hat_one_grad)
    sum_one = bias_sums(gh, val)

    def emit_carried_one(c, conv):
        rows[pl.ds(c, SEQ, stride=COLS), :] = (
            b1_ref[base + c] * gh[:, lanes(c)].astype(f32) + rnd(conv)
        )

    inverse(hat1, hat_one_grad, True, emit_carried_one)
    weight_rows(0, (sum_one, sum_two))
    for i in range(1, DP):
        k_copy(0, i).start()

    inverse(hath, hatg, True, emit_gf(1))
    gf_all[1, d] = gf_s[1, d]
    for i in range(1, DP):
        h_copy(1, i).start()

    received(gw_in.at[0:DP - 1, part_rows(1)], kr.at[1], friend)
    total_rows(1)
    for i in FAR:
        wz_copy(1, i).start()
    inverse(hatv, hat_one_grad, True, emit_gf(0))
    gf_all[0, d] = gf_s[0, d]
    for i in range(1, DP):
        h_copy(0, i).start()

    received(gw_in.at[0:DP - 1, part_rows(0)], kr.at[0], friend)
    total_rows(0)
    for i in FAR:
        wz_copy(0, i).start()
    keep_out.wait()
    received(out_mid.at[0:SEQ // 2 - 1], or_.at[0], friend)
    near_copy(out_mid, outg_ref, 1, os_, or_).start()
    keep_plane = pltpu.make_async_copy(out_mid.at[:, core], outg_ref.at[:, core], loc.at[5])
    keep_plane.start()

    def turn(k):
        block = []
        for n in range(SEQ):
            b = gw_g[n // 2, n % 2].astype(f32)
            tiles = [b[r:r + 8] for r in range(0, 24, 8)]
            if k == 1:
                block += [tiles[0], pltpu.roll(tiles[0], EVENTS, 1), tiles[1]]
            else:
                block += [
                    pltpu.roll(tiles[1], EVENTS, 1), tiles[2], pltpu.roll(tiles[2], EVENTS, 1)
                ]
        for p in range(D // TILE):
            turned = jnp.concatenate(block[16 * p:16 * p + 16], axis=0).T
            at = (k - 1) * D + p * TILE
            gw_o[:, at:at + TILE] = turned[0:EVENTS, :]

    def pass_weights(part):
        received(gw_all[part].at[0:SEQ // 2 - 1, 0], wr.at[part], friend)
        wg_copy(part).start()

    pass_weights(1)
    finish_filter(1, gf2_ref)
    received(gw_all[1].at[:, 0], wr.at[3], friend)
    turn(1)
    turn(2)
    give(gw_o, gwo_ref, 2)
    pass_weights(0)
    give(gw_v.at[:, core], gwv_ref.at[:, core], 3)
    finish_filter(0, gf1_ref)
    received(gw_v.at[:, 0], wr.at[2], friend)
    keep_plane.wait()
    received(outg_ref.at[:, 0], or_.at[1], friend)
    sent(lev_ref.at[0, 0:ZN - 1], zs.at[0], friend)
    sent(lev_ref.at[0:GROUP - 1], gs.at[0], friend)
    sent(f1_ref.at[0:DP - 1], fs.at[0], friend)
    sent(f2_ref.at[0:DP - 1], fs.at[1], friend)
    sent(cot_mid.at[0:SEQ // 2 - 1], cs.at[0], friend)
    sent(cot_ref.at[:, 0], cs.at[1], friend)
    sent(out_mid.at[0:SEQ // 2 - 1], os_.at[0], friend)
    sent(outg_ref.at[:, 0], os_.at[1], friend)
    for part in range(2):
        sent(gf_all.at[part, 0:DP - 1], hs.at[part], friend)
        sent(gw_in.at[0:DP - 1, part_rows(part)], ks.at[part], friend)
        sent(gw_all[part].at[0:SEQ // 2 - 1, 0], ws.at[part], friend)
        sent(gw_all[part].at[:, 0], ws.at[2 + part], friend)
    for copy in gives:
        copy.wait()


def whole(counts, w_in, b1, b2, cot, f1, f2):
    dma = pltpu.SemaphoreType.DMA
    vm = pltpu.VMEM
    spec = (SEQ * CH, 2 * TILE)
    return pl.pallas_call(
        whole_kernel,
        out_shape=(
            jax.ShapeDtypeStruct((SEQ // 2, 2, CH, TILE), bf16),
            jax.ShapeDtypeStruct((3, BINS), bf16),
            jax.ShapeDtypeStruct((3, BINS), bf16),
            jax.ShapeDtypeStruct((EVENTS, 2 * D), f32),
            jax.ShapeDtypeStruct((SEQ // 2, 2, 16, TILE), bf16),
        ),
        in_specs=[ANY] * 8,
        out_specs=(ANY,) * 5,
        scratch_shapes=[
            vm((EVENTS, TILE), jnp.int32),
            vm((EVENTS, 3 * D), bf16),
            vm((640, 2 * TILE), f32),
            pltpu.SMEM((D,), f32),
            pltpu.SMEM((D,), f32),
            vm((2 * SEQ, 2 * SEQ), bf16),
            vm((4 * TILE, 2 * TILE), bf16),
            vm((4 * TILE, 2 * TILE), bf16),
            vm((SEQ, 4 * SEQ), bf16),
            vm((2, SEQ, TILE), f32),
            vm((EVENTS, TILE), bf16),
            vm((3 * D, EVENTS), f32),
            vm((COLS, EVENTS), bf16),
            vm((GROUP, ZN, EVENTS, TILE), bf16),
            vm((SEQ // 2, 2, CH, TILE), bf16),
            vm((SEQ // 2, 2, CH, TILE), bf16),
            vm((DP, CH, BINS // DP), bf16),
            vm((DP, CH, BINS // DP), bf16),
            vm((TILE, BINS), bf16),
            vm((SEQ * COLS, TILE), f32),
            vm((SEQ * CH, TILE), f32),
            vm((SEQ, LANES), bf16),
            vm((SEQ, LANES), bf16),
            vm((SEQ, LANES), bf16),
            vm((SEQ, LANES), bf16),
            vm((SEQ, LANES), bf16),
            vm((SEQ, LANES), f32),
            vm((SEQ, LANES), f32),
            vm((SEQ, LANES), bf16),
            vm((SEQ * CH, 2 * TILE), bf16),
            vm(spec, f32),
            vm(spec, f32),
            vm(spec, f32),
            vm(spec, f32),
            vm(spec, f32),
            vm(spec, f32),
            vm(spec, f32),
            vm((COLS, BINS), bf16),
            vm((SEQ // 2, 2, CH, TILE), bf16),
            vm((SEQ // 2, 2, CH, TILE), bf16),
            vm((2, DP, SEQ, 3 * TILE), bf16),
            vm((40, TILE), f32),
            vm((2, DP, SEQ, 3 * TILE), bf16),
            vm((DP, 40, TILE), f32),
            vm((SEQ // 2, 2, 16, TILE), bf16),
            vm((SEQ // 2, 2, 24, TILE), bf16),
            vm((8, BINS), f32),
            vm((2, 3, BINS), bf16),
            vm((EVENTS, 2 * D), f32),
            dma((5,)),
            dma((6,)),
            dma((6,)),
            dma((8,)),
            dma((8,)),
            dma((1,)),
            dma((1,)),
            dma((1,)),
            dma((2,)),
            dma((4,)),
            dma((2,)),
            dma((2,)),
            dma((2,)),
            dma((2,)),
            dma((2,)),
            dma((2,)),
            dma((2,)),
            dma((2,)),
            dma((4,)),
            dma((4,)),
        ],
        compiler_params=pltpu.CompilerParams(
            collective_id=0, has_side_effects=True, vmem_limit_bytes=LIMIT
        ),
        name="whole",
    )(counts, w_in, b1, b2, cot, f1, f2, tables())


def finish_kernel(
    out_in, gf1_in, gf2_in, gates_in, value_in,
    out_ref, gf1_ref, gf2_ref, gw_ref, gb1_ref, gb2_ref,
):
    low = lax.broadcasted_iota(jnp.int32, (8, TILE), 1) < EVENTS
    block = []
    for n in range(SEQ):
        b = value_in[n // 2, n % 2].astype(f32)
        first, last = b[0:8], b[8:16]
        block.append(jnp.where(low, first, last))
        block.append(
            jnp.where(low, pltpu.roll(first, EVENTS, 1), pltpu.roll(last, TILE - 1, 1))
        )
        block.append(jnp.where(low, last, pltpu.roll(last, TILE - 2, 1)))
    for p in range(D // TILE):
        turned = jnp.concatenate(block[16 * p:16 * p + 16], axis=0).T
        at = slice(p * TILE, (p + 1) * TILE)
        gw_ref[:, at] = turned[0:EVENTS, :]
        gb1_ref[at] = turned[EVENTS]
        gb2_ref[at] = turned[EVENTS + 3]
    gw_ref[:, D:] = gates_in[...]
    out_ref[...] = out_in[...]
    gf1_ref[...] = gf1_in[...]
    gf2_ref[...] = gf2_in[...]


def finish(out, gf1, gf2, gates, value):
    def like(x):
        return jax.ShapeDtypeStruct(x.shape, x.dtype)

    flat = jax.ShapeDtypeStruct((D,), f32)
    return pl.pallas_call(
        finish_kernel,
        out_shape=(
            like(out), like(gf1), like(gf2), jax.ShapeDtypeStruct((EVENTS, 3 * D), f32), flat, flat
        ),
        in_specs=[VMEM] * 5,
        out_specs=(VMEM,) * 6,
        compiler_params=pltpu.CompilerParams(vmem_limit_bytes=LIMIT),
        name="finish",
    )(out, gf1, gf2, gates, value)


def body(counts, w_in, bias_one, bias_two, filter_one, filter_two, cotangent):
    out, gf1, gf2, gates, value = whole(
        counts[0].T, w_in, bias_one, bias_two, cotangent.reshape(SEQ // 2, 2, CH, TILE),
        filter_one, filter_two,
    )
    out, gf1, gf2, gw, gb1, gb2 = finish(out.reshape(1, D, TILE), gf1, gf2, gates, value)
    return out, gw, gb1, gb2, gf1, gf2


def solution(mesh):
    return jax.shard_map(
        body,
        mesh=mesh,
        in_specs=(
            P("dp", "seq", None),
            P(),
            P(),
            P(),
            P("seq", "dp"),
            P("seq", "dp"),
            P("dp", None, "seq"),
        ),
        out_specs=(
            P("dp", None, "seq"),
            P(),
            P(),
            P(),
            P(("seq", "dp"), None),
            P(("seq", "dp"), None),
        ),
        check_vma=False,
    )
```
